512 devices in a mesh: rows: 64 (over y, z_lo, core), cols: 8 (over x, z_hi).
Axes of the slice: x: 4, y: 8, z: 8 (z_hi: 2, z_lo: 4; z = z_hi * 4 + z_lo), core: 2. Of those that a mesh axis runs over, the one named last changes fastest.
Arguments:
- grad_out: bfloat16 [65536, 256], P(('rows', 'cols')), may hold values from -6 to 6
- mask_top: int32 [65536, 256], P(('rows', 'cols')), may hold values 0 or 1
- mask_mid: int32 [65536, 256], P(('rows', 'cols')), may hold values 0 or 1
- feats_in: bfloat16 [65536, 256], P(('rows', 'cols')), may hold values from -6 to 6
- feats_mid: bfloat16 [65536, 256], P(('rows', 'cols')), may hold values from -6 to 6
- weight_first: bfloat16 [256, 256], replicated, may hold values from -0.375 to 0.375
- weight_second: bfloat16 [256, 256], replicated, may hold values from -0.375 to 0.375
- adj_blocks: bfloat16 [512, 8, 12, 128, 128], P('rows', 'cols'), may hold values from -0.3125 to 0.3125
- block_cols: int32 [512, 8, 12], P('rows', 'cols'), may hold values from 0 to 63
- block_counts: int32 [512, 8], P('rows', 'cols'), may hold values from 1 to 12, as said below
Outputs:
- grad_in: bfloat16 [65536, 256], P(('rows', 'cols'))
- grad_first: float32 [256, 256], replicated
- grad_second: float32 [256, 256], replicated
The draws below stay inside these ranges and needn't reach their ends.
Inputs may be any that keep to these rules, and one draw needn't show every extreme that they name: `block_counts`: in some row group (the 8 row blocks held by one device index along rows) the counts run higher than in others; some entry equals 12.
All inputs are finite; a program needn't handle non-finite values. No bound on the sum of `mask_top` or of `mask_mid` on one device may be relied on, other than what follows from the above.
Results may differ from the reference program's by a relative error of at most 0.0075.
Values may be sent and summed in bfloat16 or wider, within the bound.
No kernel may reach another device: no remote copies, remote signals or barrier semaphores. Data moves between devices by JAX's collectives and lax.ppermute only.
A program may use at most 64 MiB of HBM per device.

```python
import jax
import jax.numpy as jnp
from jax import lax

F = 256
BS = 128
MAXNB = 12
BLK_DEV = 1
NB = 512
NODES = 65536
PART_BLOCKS = 64
N_ROWS = 64
N_COLS = 8


def draw_block_counts(key, part):
    key = jax.random.fold_in(key, 5)
    key_level, key_count, key_spot = jax.random.split(key, 3)
    levels = jax.random.randint(key_level, (N_ROWS,), 1, MAXNB + 1)
    levels = jnp.maximum(1, levels * levels // MAXNB)
    group_ids = jnp.arange(NB, dtype=jnp.int32) // (N_COLS * BLK_DEV)
    ceiling = levels[group_ids][:, None]
    raw_values = jax.random.randint(key_count, (NB, N_COLS), 0, 1 << 20)
    counted = raw_values % ceiling + 1
    spot = jax.random.randint(key_spot, (), 0, NB * N_COLS)
    flat_ids = jnp.arange(NB * N_COLS, dtype=jnp.int32).reshape(NB, N_COLS)
    return jnp.where(flat_ids == spot, MAXNB, counted).astype(jnp.int32)


def plant(entries, own_key, low, top_value):
    index_at = [jax.random.randint(jax.random.fold_in(own_key, axis), (), 0, length) for axis, length in enumerate(entries.shape)]
    main_axis = entries.shape.index(max(entries.shape))
    next_to = index_at[:main_axis] + [(index_at[main_axis] + 1) % entries.shape[main_axis]] + index_at[main_axis + 1:]
    return entries.at[tuple(index_at)].set(low).at[tuple(next_to)].set(top_value)


def block_scale(own_key, extent, cuts, low, top_value):
    loudness, own = 1.0, jax.random.fold_in(own_key, 6)
    for position, parts in cuts:
        heights = jnp.exp(jax.random.uniform(jax.random.fold_in(own, position), (parts,), jnp.float32, low / len(cuts), top_value / len(cuts)))
        loudness = loudness * jnp.repeat(heights, extent[position] // parts).reshape([-1 if axis == position else 1 for axis in range(len(extent))])
    return loudness


def centred(own_key, dims, width, reach, pieces=(), kind=jnp.bfloat16):
    array = width * jax.random.normal(own_key, dims, jnp.float32)
    if pieces:
        array = array * block_scale(own_key, dims, pieces, -0.22, 0.18)
    return jnp.clip(array, -reach, reach).astype(kind)


def setup_inputs(seed: int = 0) -> dict:
    seeds = jax.random.split(jax.random.key(seed), 11)
    grad_out = centred(seeds[0], (NODES, F), 1.0, 6.0, ((0, 512),))
    mask_top = plant((jax.random.randint(seeds[1], (NODES, F), 0, 2) < 1).astype(jnp.int32), jax.random.fold_in(seeds[1], 1), 0, 1)
    mask_mid = plant((jax.random.randint(seeds[2], (NODES, F), 0, 2) < 1).astype(jnp.int32), jax.random.fold_in(seeds[2], 1), 0, 1)
    feats_in = centred(seeds[3], (NODES, F), 1.0, 6.0, ((0, 512),))
    feats_mid = centred(seeds[4], (NODES, F), 1.0, 6.0, ((0, 512),))
    weight_first = centred(seeds[5], (F, F), F ** -0.5, 0.375)
    weight_second = centred(seeds[6], (F, F), F ** -0.5, 0.375)
    adj_blocks = centred(seeds[7], (NB, N_COLS, MAXNB, BS, BS), 0.05, 0.3125, ((0, 64), (1, 8)))
    block_cols = plant(jax.random.randint(seeds[8], (NB, N_COLS, MAXNB), 0, PART_BLOCKS), jax.random.fold_in(seeds[8], 1), 0, PART_BLOCKS - 1).astype(jnp.int32)
    block_counts = draw_block_counts(jax.random.fold_in(seeds[10], 71), 0)
    return dict(grad_out=grad_out, mask_top=mask_top, mask_mid=mask_mid, feats_in=feats_in, feats_mid=feats_mid, weight_first=weight_first, weight_second=weight_second, adj_blocks=adj_blocks, block_cols=block_cols, block_counts=block_counts)


def apply_blocks(values, adj_blocks, block_cols, block_counts):
    node_blocks = values.reshape(NB, BS, F)
    owners = block_cols // BLK_DEV
    within = block_cols % BLK_DEV
    part_ids = jnp.arange(N_COLS, dtype=jnp.int32)[None, :, None]
    global_ids = ((owners * N_COLS + part_ids) * BLK_DEV + within).astype(jnp.int32)
    live_slot = jnp.arange(MAXNB, dtype=jnp.int32)[None, None, :] < block_counts[:, :, None]

    def one_block(item):
        block_rows, targets, alive = item
        chosen = node_blocks[targets]
        chosen = jnp.where(alive[:, :, None, None], chosen, jnp.zeros_like(chosen))
        return jnp.einsum('ckab,ckbf->af', block_rows.astype(jnp.float32), chosen.astype(jnp.float32))
    summed = lax.map(one_block, (adj_blocks, global_ids, live_slot))
    return summed.reshape(NODES, F).astype(jnp.bfloat16)

def reference(grad_out, mask_top, mask_mid, feats_in, feats_mid, weight_first, weight_second, adj_blocks, block_cols, block_counts):
    norm_scale = 1.0 / jnp.sqrt(jnp.float32(NODES))
    grad_top = jnp.where(mask_top > 0, grad_out, jnp.zeros_like(grad_out))
    agg_top = apply_blocks(grad_top, adj_blocks, block_cols, block_counts)
    grad_second = jnp.dot(feats_mid.T, agg_top, preferred_element_type=jnp.float32) * norm_scale
    hidden_grad = jnp.dot(agg_top, weight_second.T, preferred_element_type=jnp.float32)
    grad_mid = jnp.where(mask_mid > 0, hidden_grad, jnp.zeros_like(hidden_grad)).astype(jnp.bfloat16)
    agg_mid = apply_blocks(grad_mid, adj_blocks, block_cols, block_counts)
    grad_first = jnp.dot(feats_in.T, agg_mid, preferred_element_type=jnp.float32) * norm_scale
    grad_in = jnp.dot(agg_mid, weight_first.T, preferred_element_type=jnp.float32).astype(jnp.bfloat16)
    return (grad_in, grad_first, grad_second)
```

```python
import jax
import jax.numpy as jnp
import numpy as np
from jax import lax
from jax.experimental import pallas as pl
from jax.experimental.pallas import tpu as pltpu
from jax.sharding import Mesh, PartitionSpec as P

Y, ZL, CORE, X, ZH = 8, 4, 2, 4, 2
AXES = ("y", "zl", "core", "x", "zh")
ROWS = ("y", "zl", "core")
COLS = ("x", "zh")
NCOL = X * ZH
BF16, F32 = jnp.bfloat16, jnp.float32


def everyone(value, axes, count):
    return lax.all_to_all(
        jnp.broadcast_to(value[None], (count,) + value.shape), axes, 0, 0, tiled=True
    )


def spmm_kernel(meta_ref, core_ref, x_ref, own_ref, other_ref, out_ref):
    core = core_ref[0]
    slots = own_ref.shape[1]
    group = 4
    for side, adj_ref in ((0, own_ref), (1, other_ref)):
        j = jnp.bitwise_xor(core, side)
        for i in range(own_ref.shape[0]):
            base = (j * own_ref.shape[0] + i) * 16
            count = meta_ref[base + slots]

            def step(s, acc, base=base, count=count, i=i, adj_ref=adj_ref):
                for t in range(group):
                    k = s * group + t
                    block = x_ref[meta_ref[base + k]]
                    block = jnp.where(k < count, block, jnp.zeros_like(block))
                    acc = acc + jnp.dot(adj_ref[i, k], block, preferred_element_type=F32)
                return acc

            acc = lax.fori_loop(
                0, (count + group - 1) // group, step, jnp.zeros(out_ref.shape[2:], F32)
            )
            out_ref[i, j] = acc.astype(out_ref.dtype)


def spmm(meta, core, gathered, own, other):
    vmem = pl.BlockSpec(memory_space=pltpu.VMEM)
    smem = pl.BlockSpec(memory_space=pltpu.SMEM)
    return pl.pallas_call(
        spmm_kernel,
        out_shape=jax.ShapeDtypeStruct((NCOL, CORE) + gathered.shape[1:], BF16),
        in_specs=[smem, smem, vmem, vmem, vmem],
        out_specs=vmem,
        compiler_params=pltpu.CompilerParams(vmem_limit_bytes=40 * 1024 * 1024),
    )(meta, core, gathered, own, other)


def contract_rows(a, b):
    return lax.dot_general(a, b, (((0,), (0,)), ((), ())), preferred_element_type=F32)


def times_transpose(a, b):
    return lax.dot_general(a, b, (((1,), (1,)), ((), ())), preferred_element_type=F32)


def local(
    grad_out, mask_top, mask_mid, feats_in, feats_mid, weight_first, weight_second,
    adj_blocks, block_cols, block_counts,
):
    bs, feats = grad_out.shape
    half = feats // CORE
    core = lax.axis_index("core")
    nodes = bs * Y * ZL * CORE * X * ZH
    norm_scale = 1.0 / jnp.sqrt(F32(nodes))

    def my_half(v):
        return lax.dynamic_slice_in_dim(v, core * half, half, axis=v.ndim - 1)

    adj = adj_blocks[:, 0]
    other_adj = lax.ppermute(adj, "core", [(0, 1), (1, 0)])
    meta = jnp.concatenate(
        [block_cols[:, 0], block_counts, jnp.zeros((NCOL, 16 - 13), jnp.int32)], axis=1
    )
    meta = lax.all_gather(meta, "core", axis=0, tiled=True).reshape(-1)
    core_id = core.astype(jnp.int32).reshape(1)

    with jax.named_scope("pair_inputs"):
        grad_top = jnp.where(mask_top > 0, grad_out, jnp.zeros_like(grad_out))
        pair = lax.all_gather(
            jnp.stack([grad_top, mask_mid.astype(BF16), feats_mid]), "core", axis=0
        )
        unit_top = my_half(pair[:, 0]).reshape(CORE * bs, half)
        mask_pair = my_half(pair[:, 1]).reshape(CORE * bs, half)
        feats_mid_pair = pair[:, 2].reshape(CORE * bs, feats)
    with jax.named_scope("group_feats"):
        feats_in_group = lax.all_gather(feats_in, ("x", "zh", "core"), axis=0, tiled=True)

    def gather_units(unit):
        return everyone(unit, ("y", "zl"), Y * ZL).reshape(-1, bs, half)

    with jax.named_scope("section_top"):
        partial_top = spmm(meta, core_id, gather_units(unit_top), adj, other_adj)
        parts = lax.all_to_all(
            partial_top.reshape(NCOL, CORE * bs, half), COLS, 0, 0, tiled=True
        )
        agg_top = jnp.sum(parts.astype(F32), axis=0).astype(BF16)
        agg_top_both = lax.all_gather(agg_top, "core", axis=1, tiled=True)
        term_second = contract_rows(feats_mid_pair, agg_top)
        weight_half = lax.dynamic_slice_in_dim(weight_second, core * half, half, axis=0)
        hidden = times_transpose(agg_top_both, weight_half)
        grad_mid = jnp.where(mask_pair > 0, hidden, jnp.zeros_like(hidden)).astype(BF16)
    with jax.named_scope("section_mid"):
        partial_mid = spmm(meta, core_id, gather_units(grad_mid), adj, other_adj)
        term_first = contract_rows(feats_in_group, partial_mid.reshape(-1, half))
        terms = jnp.stack([term_first, term_second]).astype(BF16)
        terms = terms.reshape(2, NCOL, feats // NCOL, half).transpose(1, 0, 2, 3)
        sent = jnp.concatenate(
            [partial_mid.reshape(NCOL, CORE * bs, half), terms.reshape(NCOL, -1, half)], axis=1
        )
        parts = lax.all_to_all(sent, COLS, 0, 0, tiled=True)
        summed = jnp.sum(parts.astype(F32), axis=0)
        agg_mid = summed[: CORE * bs].astype(BF16)
        own_nodes = lax.all_gather(agg_mid, "core", axis=1, tiled=True)
        own_nodes = lax.dynamic_slice_in_dim(own_nodes, core * bs, bs, axis=0)
        grad_in = times_transpose(own_nodes, weight_first).astype(BF16)
    with jax.named_scope("weight_sums"):
        piece = summed[CORE * bs :]
        over_z = everyone(piece.astype(BF16), ("zh", "zl"), ZH * ZL)
        piece = jnp.sum(over_z.reshape((ZH, ZL) + piece.shape).astype(F32), axis=1)
        over_y = everyone(piece.astype(BF16), "y", Y)
        piece = jnp.sum(over_y.reshape((Y,) + piece.shape).astype(F32), axis=0)
        over_x = everyone(piece, "x", X).reshape(NCOL, 2, feats // NCOL, half)
        whole = lax.all_gather(over_x * norm_scale, "core", axis=3, tiled=True)
        whole = whole.transpose(1, 0, 2, 3).reshape(2, feats, feats)
    return (grad_in, whole[0], whole[1])


def solution(mesh):
    parts = Mesh(mesh.devices.reshape(Y, ZL, CORE, X, ZH), AXES)
    nodes = P(AXES, None)
    return jax.shard_map(
        local,
        mesh=parts,
        in_specs=(
            nodes, nodes, nodes, nodes, nodes, P(), P(),
            P(ROWS, COLS, None, None, None),
            P(ROWS, COLS, None),
            P(ROWS, COLS),
        ),
        out_specs=(nodes, P(), P()),
        check_vma=False,
    )
```

```python
import jax
import jax.numpy as jnp
import numpy as np
from jax import lax
from jax.experimental import pallas as pl
from jax.experimental.pallas import tpu as pltpu
from jax.sharding import Mesh, PartitionSpec as P

Y, ZL, CORE, X, ZH = 8, 4, 2, 4, 2
AXES = ("y", "zl", "core", "x", "zh")
ROWS = ("y", "zl", "core")
COLS = ("x", "zh")
NCOL = X * ZH
BF16, F32 = jnp.bfloat16, jnp.float32


def everyone(value, axes, count):
    return lax.all_to_all(
        jnp.broadcast_to(value[None], (count,) + value.shape), axes, 0, 0, tiled=True
    )


def y_pairs(which):
    pairs = []
    for y in range(Y):
        for core in range(CORE):
            up = (y + core + which) % 2 == 0
            pairs.append((y * CORE + core, (y + (1 if up else -1)) % Y * CORE + core))
    return pairs


def piece_table():
    step = [dict(y_pairs(0)), dict(y_pairs(1))]
    table = np.zeros((Y * CORE, Y), np.int32)
    for me in range(Y * CORE):
        for piece, hops in enumerate(
            ((), (0,), (1,), (1, 0), (0, 1), (0, 1, 0), (1, 0, 1), (1, 0, 1, 0))
        ):
            at = me
            for hop in hops:
                at = step[hop][at]
            table[me, at // CORE] = piece
    return table


def gather_y(mine):
    def swap(value, which):
        return lax.ppermute(value, ("y", "core"), y_pairs(which))

    first, second = swap(mine, 0), swap(mine, 1)
    third, fourth = swap(first, 1), swap(second, 0)
    fifth, sixth = swap(third, 0), swap(fourth, 1)
    last = swap(fifth, 1)
    return mine, first, second, third, fourth, fifth, sixth, last


def spmm_kernel(meta_ref, core_ref, *refs):
    pieces, (own_ref, other_ref, out_ref, x_ref, adj_ref, x_sem, adj_sem) = refs[:Y], refs[Y:]
    core = core_ref[0]
    per_side, slots = own_ref.shape[0], own_ref.shape[1]
    per_piece = pieces[0].shape[0]
    group = 4
    x_copies = [
        pltpu.make_async_copy(ref, x_ref.at[pl.ds(p * per_piece, per_piece)], x_sem.at[p])
        for p, ref in enumerate(pieces)
    ]
    adj_copies = [
        pltpu.make_async_copy(ref.at[i], adj_ref.at[side * per_side + i], adj_sem.at[side * per_side + i])
        for side, ref in enumerate((own_ref, other_ref))
        for i in range(per_side)
    ]
    for copy in x_copies + adj_copies:
        copy.start()
    for copy in x_copies:
        copy.wait()
    for n, copy in enumerate(adj_copies):
        side, i = divmod(n, per_side)
        j = jnp.bitwise_xor(core, side)
        base = (j * per_side + i) * 16
        count = meta_ref[base + slots]
        copy.wait()

        def step(s, acc, base=base, count=count, n=n):
            blocks = []
            for t in range(group):
                k = s * group + t
                block = x_ref[meta_ref[base + k]]
                blocks.append(jnp.where(k < count, block, jnp.zeros_like(block)))
            adj = [adj_ref[n, s * group + t] for t in range(group)]
            return acc + jnp.dot(
                jnp.concatenate(adj, axis=1),
                jnp.concatenate(blocks, axis=0),
                preferred_element_type=F32,
            )

        acc = lax.fori_loop(
            0, (count + group - 1) // group, step, jnp.zeros(out_ref.shape[2:], F32)
        )
        out_ref[i, j] = acc.astype(out_ref.dtype)


def spmm(meta, core, pieces, own, other):
    smem = pl.BlockSpec(memory_space=pltpu.SMEM)
    anywhere = pl.BlockSpec(memory_space=pl.ANY)
    blocks, bs, half = pieces[0].shape
    rows = own.shape[0] * CORE
    return pl.pallas_call(
        spmm_kernel,
        out_shape=jax.ShapeDtypeStruct((NCOL, CORE, bs, half), BF16),
        in_specs=[smem, smem] + [anywhere] * (Y + 2),
        out_specs=pl.BlockSpec(memory_space=pltpu.VMEM),
        scratch_shapes=[
            pltpu.VMEM((blocks * Y, bs, half), BF16),
            pltpu.VMEM((rows,) + own.shape[1:], BF16),
            pltpu.SemaphoreType.DMA((Y,)),
            pltpu.SemaphoreType.DMA((rows,)),
        ],
        compiler_params=pltpu.CompilerParams(vmem_limit_bytes=20 * 1024 * 1024),
    )(meta, core, *pieces, own, other)


def contract_rows(a, b):
    return lax.dot_general(a, b, (((0,), (0,)), ((), ())), preferred_element_type=F32)


def times_transpose(a, b):
    return lax.dot_general(a, b, (((1,), (1,)), ((), ())), preferred_element_type=F32)


def local(
    grad_out, mask_top, mask_mid, feats_in, feats_mid, weight_first, weight_second,
    adj_blocks, block_cols, block_counts,
):
    bs, feats = grad_out.shape
    half = feats // CORE
    core = lax.axis_index("core")
    nodes = bs * Y * ZL * CORE * X * ZH
    norm_scale = 1.0 / jnp.sqrt(F32(nodes))

    def my_half(v):
        return lax.dynamic_slice_in_dim(v, core * half, half, axis=v.ndim - 1)

    adj = adj_blocks[:, 0]
    other_adj = lax.ppermute(adj, "core", [(0, 1), (1, 0)])
    meta = jnp.concatenate(
        [block_cols[:, 0], block_counts, jnp.zeros((NCOL, 16 - 13), jnp.int32)], axis=1
    )
    meta = lax.all_gather(meta, "core", axis=0, tiled=True).reshape(-1)
    row = lax.dynamic_slice_in_dim(
        jnp.asarray(piece_table()), lax.axis_index("y") * CORE + core, 1, axis=0
    )[0]
    per_piece = ZL * CORE
    place = sum(
        jnp.where(meta // per_piece == y, row[y] * per_piece, 0) for y in range(Y)
    ) + meta % per_piece
    is_count = jnp.arange(meta.shape[0]) % 16 == 12
    meta = jnp.where(is_count, meta, place)
    core_id = core.astype(jnp.int32).reshape(1)

    with jax.named_scope("pair_inputs"):
        grad_top = jnp.where(mask_top > 0, grad_out, jnp.zeros_like(grad_out))
        unit_top = my_half(lax.all_gather(grad_top, "core", axis=0, tiled=True))
        pair = lax.all_gather(jnp.stack([mask_mid.astype(BF16), feats_mid]), "core", axis=1, tiled=True)
        mask_pair = my_half(pair[0])
        feats_mid_pair = pair[1]
    with jax.named_scope("group_feats"):
        feats_in_group = lax.all_gather(feats_in, ("x", "zh", "core"), axis=0, tiled=True)

    def gather_units(unit):
        return gather_y(everyone(unit, "zl", ZL).reshape(-1, bs, half))

    with jax.named_scope("section_top"):
        partial_top = spmm(meta, core_id, gather_units(unit_top), adj, other_adj)
        parts = lax.all_to_all(
            partial_top.reshape(NCOL, CORE * bs, half), COLS, 0, 0, tiled=True
        )
        parts, feats_in_group = lax.optimization_barrier((parts, feats_in_group))
        agg_top = jnp.sum(parts.astype(F32), axis=0).astype(BF16)
        agg_top_both = lax.all_gather(agg_top, "core", axis=1, tiled=True)
        term_second = contract_rows(feats_mid_pair, agg_top)
        weight_half = lax.dynamic_slice_in_dim(weight_second, core * half, half, axis=0)
        hidden = times_transpose(agg_top_both, weight_half)
        grad_mid = jnp.where(mask_pair > 0, hidden, jnp.zeros_like(hidden)).astype(BF16)
    with jax.named_scope("section_mid"):
        partial_mid = spmm(meta, core_id, gather_units(grad_mid), adj, other_adj)
        term_first = contract_rows(feats_in_group, partial_mid.reshape(-1, half))
        terms = jnp.stack([term_first, term_second]).astype(BF16)
        terms = terms.reshape(2, NCOL, feats // NCOL, half).transpose(1, 0, 2, 3)
        sent = jnp.concatenate(
            [partial_mid.reshape(NCOL, CORE * bs, half), terms.reshape(NCOL, -1, half)], axis=1
        )
        parts = lax.all_to_all(sent, COLS, 0, 0, tiled=True)
        summed = jnp.sum(parts.astype(F32), axis=0)
        agg_mid = summed[: CORE * bs].astype(BF16)
        own_nodes = lax.all_gather(agg_mid, "core", axis=1, tiled=True)
        own_nodes = lax.dynamic_slice_in_dim(own_nodes, core * bs, bs, axis=0)
        grad_in = times_transpose(own_nodes, weight_first).astype(BF16)
    with jax.named_scope("weight_sums"):
        piece = summed[CORE * bs :]
        over_z = everyone(piece.astype(BF16), ("zh", "zl"), ZH * ZL)
        piece = jnp.sum(over_z.reshape((ZH, ZL) + piece.shape).astype(F32), axis=1)
        over_y = everyone(piece.astype(BF16), "y", Y)
        piece = jnp.sum(over_y.reshape((Y,) + piece.shape).astype(F32), axis=0)
        over_x = everyone(piece, "x", X).reshape(NCOL, 2, feats // NCOL, half)
        whole = lax.all_gather(over_x * norm_scale, "core", axis=3, tiled=True)
        whole = whole.transpose(1, 0, 2, 3).reshape(2, feats, feats)
    return (grad_in, whole[0], whole[1])


def solution(mesh):
    parts = Mesh(mesh.devices.reshape(Y, ZL, CORE, X, ZH), AXES)
    nodes = P(AXES, None)
    return jax.shard_map(
        local,
        mesh=parts,
        in_specs=(
            nodes, nodes, nodes, nodes, nodes, P(), P(),
            P(ROWS, COLS, None, None, None),
            P(ROWS, COLS, None),
            P(ROWS, COLS),
        ),
        out_specs=(nodes, P(), P()),
        check_vma=False,
    )
```

```python
import jax
import jax.numpy as jnp
import numpy as np
from jax import lax
from jax.experimental import pallas as pl
from jax.experimental.pallas import tpu as pltpu
from jax.sharding import Mesh, PartitionSpec as P

Y, ZL, CORE, X, ZH = 8, 4, 2, 4, 2
AXES = ("y", "zl", "core", "x", "zh")
ROWS = ("y", "zl", "core")
COLS = ("x", "zh")
NCOL = X * ZH
BF16, F32 = jnp.bfloat16, jnp.float32


def everyone(value, axes, count):
    return lax.all_to_all(
        jnp.broadcast_to(value[None], (count,) + value.shape), axes, 0, 0, tiled=True
    )


def y_pairs(which):
    pairs = []
    for y in range(Y):
        for core in range(CORE):
            up = (y + core + which) % 2 == 0
            pairs.append((y * CORE + core, (y + (1 if up else -1)) % Y * CORE + core))
    return pairs


def piece_table():
    step = [dict(y_pairs(0)), dict(y_pairs(1))]
    table = np.zeros((Y * CORE, Y), np.int32)
    for me in range(Y * CORE):
        for piece, hops in enumerate(
            ((), (0,), (1,), (1, 0), (0, 1), (0, 1, 0), (1, 0, 1), (1, 0, 1, 0))
        ):
            at = me
            for hop in hops:
                at = step[hop][at]
            table[me, at // CORE] = piece
    return table


def gather_y(mine):
    def swap(value, which):
        return lax.ppermute(value, ("y", "core"), y_pairs(which))

    first, second = swap(mine, 0), swap(mine, 1)
    third, fourth = swap(first, 1), swap(second, 0)
    fifth, sixth = swap(third, 0), swap(fourth, 1)
    last = swap(fifth, 1)
    return mine, first, second, third, fourth, fifth, sixth, last


def spmm_kernel(meta_ref, core_ref, *refs):
    pieces, (own_ref, other_ref, out_ref, x_ref, adj_ref, x_sem, adj_sem) = refs[:Y], refs[Y:]
    core = core_ref[0]
    per_side, slots = own_ref.shape[0], own_ref.shape[1]
    per_piece = pieces[0].shape[0]
    together = 4
    groups = per_side // together
    x_copies = [
        pltpu.make_async_copy(ref, x_ref.at[pl.ds(p * per_piece, per_piece)], x_sem.at[p])
        for p, ref in enumerate(pieces)
    ]

    def adj_copy(ref, side, m):
        return pltpu.make_async_copy(
            ref.at[pl.ds(m * together, together)],
            adj_ref.at[pl.ds(side * per_side + m * together, together)],
            adj_sem.at[side * groups + m],
        )

    for copy in x_copies:
        copy.start()
    for side, ref in enumerate((own_ref, other_ref)):
        for m in range(groups):
            adj_copy(ref, side, m).start()
    for copy in x_copies:
        copy.wait()

    for side, ref in enumerate((own_ref, other_ref)):
        j = jnp.bitwise_xor(core, side)

        def some_rows(m, carry, side=side, ref=ref, j=j):
            adj_copy(ref, side, m).wait()
            for t in range(together):
                i = m * together + t
                base = (j * per_side + i) * 16
                count = meta_ref[base + slots]
                blocks = []
                for k in range(slots):
                    block = x_ref[meta_ref[base + k]]
                    blocks.append(jnp.where(k < count, block, jnp.zeros_like(block)))
                adj = [adj_ref[side * per_side + i, k] for k in range(slots)]
                out_ref[i, j] = jnp.dot(
                    jnp.concatenate(adj, axis=1),
                    jnp.concatenate(blocks, axis=0),
                    preferred_element_type=F32,
                ).astype(out_ref.dtype)
            return carry

        lax.fori_loop(0, groups, some_rows, 0)


def spmm(meta, core, pieces, own, other):
    smem = pl.BlockSpec(memory_space=pltpu.SMEM)
    anywhere = pl.BlockSpec(memory_space=pl.ANY)
    blocks, bs, half = pieces[0].shape
    rows = own.shape[0] * CORE
    return pl.pallas_call(
        spmm_kernel,
        out_shape=jax.ShapeDtypeStruct((NCOL, CORE, bs, half), BF16),
        in_specs=[smem, smem] + [anywhere] * (Y + 2),
        out_specs=pl.BlockSpec(memory_space=pltpu.VMEM),
        scratch_shapes=[
            pltpu.VMEM((blocks * Y, bs, half), BF16),
            pltpu.VMEM((rows,) + own.shape[1:], BF16),
            pltpu.SemaphoreType.DMA((Y,)),
            pltpu.SemaphoreType.DMA((rows // 4,)),
        ],
        compiler_params=pltpu.CompilerParams(vmem_limit_bytes=60 * 1024 * 1024),
    )(meta, core, *pieces, own, other)


def contract_rows(a, b):
    return lax.dot_general(a, b, (((0,), (0,)), ((), ())), preferred_element_type=F32)


def times_transpose(a, b):
    return lax.dot_general(a, b, (((1,), (1,)), ((), ())), preferred_element_type=F32)


def local(
    grad_out, mask_top, mask_mid, feats_in, feats_mid, weight_first, weight_second,
    adj_blocks, block_cols, block_counts,
):
    bs, feats = grad_out.shape
    half = feats // CORE
    core = lax.axis_index("core")
    nodes = bs * Y * ZL * CORE * X * ZH
    norm_scale = 1.0 / jnp.sqrt(F32(nodes))

    def my_half(v):
        return lax.dynamic_slice_in_dim(v, core * half, half, axis=v.ndim - 1)

    adj = adj_blocks[:, 0]
    meta = jnp.concatenate(
        [block_cols[:, 0], block_counts, jnp.zeros((NCOL, 16 - 13), jnp.int32)], axis=1
    )
    meta = lax.all_gather(meta, "core", axis=0, tiled=True).reshape(-1)
    row = lax.dynamic_slice_in_dim(
        jnp.asarray(piece_table()), lax.axis_index("y") * CORE + core, 1, axis=0
    )[0]
    per_piece = ZL * CORE
    place = sum(
        jnp.where(meta // per_piece == y, row[y] * per_piece, 0) for y in range(Y)
    ) + meta % per_piece
    is_count = jnp.arange(meta.shape[0]) % 16 == 12
    meta = jnp.where(is_count, meta, place)
    core_id = core.astype(jnp.int32).reshape(1)

    with jax.named_scope("pair_inputs"):
        grad_top = jnp.where(mask_top > 0, grad_out, jnp.zeros_like(grad_out))
        unit_top = my_half(lax.all_gather(grad_top, "core", axis=0, tiled=True))
        pair = lax.all_gather(
            jnp.stack([mask_mid.astype(BF16), feats_mid, feats_in]), "core", axis=1, tiled=True
        )
        mask_pair = my_half(pair[0])
        feats_mid_pair = pair[1]
    with jax.named_scope("group_feats"):
        feats_in_group = everyone(pair[2], COLS, NCOL).reshape(-1, feats)

    def gather_z(unit):
        return everyone(unit, "zl", ZL).reshape(-1, bs, half)

    with jax.named_scope("section_top"):
        units = gather_z(unit_top)
        adj, units = lax.optimization_barrier((adj, units))
        other_adj = lax.ppermute(adj, "core", [(0, 1), (1, 0)])
        partial_top = spmm(meta, core_id, gather_y(units), adj, other_adj)
        parts = lax.all_to_all(
            partial_top.reshape(NCOL, CORE * bs, half), COLS, 0, 0, tiled=True
        )
        agg_top = jnp.sum(parts.astype(F32), axis=0).astype(BF16)
        agg_top_both = lax.all_gather(agg_top, "core", axis=1, tiled=True)
        term_second = contract_rows(feats_mid_pair, agg_top)
        weight_half = lax.dynamic_slice_in_dim(weight_second, core * half, half, axis=0)
        hidden = times_transpose(agg_top_both, weight_half)
        grad_mid = jnp.where(mask_pair > 0, hidden, jnp.zeros_like(hidden)).astype(BF16)
    with jax.named_scope("section_mid"):
        partial_mid = spmm(meta, core_id, gather_y(gather_z(grad_mid)), adj, other_adj)
        term_first = contract_rows(feats_in_group, partial_mid.reshape(-1, half))
        terms = jnp.stack([term_first, term_second]).astype(BF16)
        terms = terms.reshape(2, NCOL, feats // NCOL, half).transpose(1, 0, 2, 3)
        sent = jnp.concatenate(
            [partial_mid.reshape(NCOL, CORE * bs, half), terms.reshape(NCOL, -1, half)], axis=1
        )
        parts = lax.all_to_all(sent, COLS, 0, 0, tiled=True)
        summed = jnp.sum(parts.astype(F32), axis=0)
        agg_mid = summed[: CORE * bs].astype(BF16)
        own_nodes = lax.all_gather(agg_mid, "core", axis=1, tiled=True)
        own_nodes = lax.dynamic_slice_in_dim(own_nodes, core * bs, bs, axis=0)
        grad_in = times_transpose(own_nodes, weight_first).astype(BF16)
    with jax.named_scope("weight_sums"):
        piece = summed[CORE * bs :]
        over_y = everyone(piece.astype(BF16), "y", Y)
        piece = jnp.sum(over_y.reshape((Y,) + piece.shape).astype(F32), axis=0)
        over_xz = everyone(piece.astype(BF16), ("x", "zh", "zl"), NCOL * ZL)
        over_x = jnp.sum(over_xz.reshape((NCOL, ZL) + piece.shape).astype(F32), axis=1)
        over_x = over_x.reshape(NCOL, 2, feats // NCOL, half)
        whole = lax.all_gather(over_x * norm_scale, "core", axis=3, tiled=True)
        whole = whole.transpose(1, 0, 2, 3).reshape(2, feats, feats)
    return (grad_in, whole[0], whole[1])


def solution(mesh):
    parts = Mesh(mesh.devices.reshape(Y, ZL, CORE, X, ZH), AXES)
    nodes = P(AXES, None)
    return jax.shard_map(
        local,
        mesh=parts,
        in_specs=(
            nodes, nodes, nodes, nodes, nodes, P(), P(),
            P(ROWS, COLS, None, None, None),
            P(ROWS, COLS, None),
            P(ROWS, COLS),
        ),
        out_specs=(nodes, P(), P()),
        check_vma=False,
    )
```

```python
import jax
import jax.numpy as jnp
import numpy as np
from jax import lax
from jax.experimental import pallas as pl
from jax.experimental.pallas import tpu as pltpu
from jax.sharding import Mesh, PartitionSpec as P

Y, ZL, CORE, X, ZH = 8, 4, 2, 4, 2
AXES = ("y", "zl", "core", "x", "zh")
ROWS = ("y", "zl", "core")
COLS = ("x", "zh")
NCOL = X * ZH
BF16, F32 = jnp.bfloat16, jnp.float32


def everyone(value, axes, count):
    return lax.all_to_all(
        jnp.broadcast_to(value[None], (count,) + value.shape), axes, 0, 0, tiled=True
    )


def y_pairs(which):
    pairs = []
    for y in range(Y):
        for core in range(CORE):
            up = (y + core + which) % 2 == 0
            pairs.append((y * CORE + core, (y + (1 if up else -1)) % Y * CORE + core))
    return pairs


def piece_table():
    step = [dict(y_pairs(0)), dict(y_pairs(1))]
    table = np.zeros((Y * CORE, Y), np.int32)
    for me in range(Y * CORE):
        for piece, hops in enumerate(
            ((), (0,), (1,), (1, 0), (0, 1), (0, 1, 0), (1, 0, 1), (1, 0, 1, 0))
        ):
            at = me
            for hop in hops:
                at = step[hop][at]
            table[me, at // CORE] = piece
    return table


def gather_y(mine, beside=None):
    def swap(value, which):
        return lax.ppermute(value, ("y", "core"), y_pairs(which))

    first, second = swap(mine, 0), swap(mine, 1)
    third, fourth = swap(first, 1), swap(second, 0)
    fifth, sixth = swap(third, 0), swap(fourth, 1)
    if beside is not None:
        fifth, beside = lax.optimization_barrier((fifth, beside))
    last = swap(fifth, 1)
    return (mine, first, second, third, fourth, fifth, sixth, last), beside


def spmm_kernel(meta_ref, table_ref, place_ref, *refs):
    pieces, (own_ref, other_ref, out_ref, x_ref, adj_ref, x_sem, adj_sem) = refs[:Y], refs[Y:]
    core = place_ref[1]
    at = (place_ref[0] * CORE + core) * Y
    per_side, slots = own_ref.shape[0], own_ref.shape[1]
    per_piece = pieces[0].shape[0]
    together = 4
    groups = per_side // together
    empty = x_ref.shape[0] - 1
    x_copies = [
        pltpu.make_async_copy(ref, x_ref.at[pl.ds(p * per_piece, per_piece)], x_sem.at[p])
        for p, ref in enumerate(pieces)
    ]

    def adj_copy(ref, side, m):
        return pltpu.make_async_copy(
            ref.at[pl.ds(m * together, together)],
            adj_ref.at[pl.ds(side * per_side + m * together, together)],
            adj_sem.at[side * groups + m],
        )

    for copy in x_copies:
        copy.start()
    for side, ref in enumerate((own_ref, other_ref)):
        for m in range(groups):
            adj_copy(ref, side, m).start()
    x_ref[empty] = jnp.zeros(x_ref.shape[1:], x_ref.dtype)
    for copy in x_copies:
        copy.wait()

    for side, ref in enumerate((own_ref, other_ref)):
        j = jnp.bitwise_xor(core, side)

        def some_rows(m, carry, side=side, ref=ref, j=j):
            adj_copy(ref, side, m).wait()
            for t in range(together):
                i = m * together + t
                base = (j * per_side + i) * 16
                count = meta_ref[base + slots]
                blocks = []
                for k in range(slots):
                    block = meta_ref[base + k]
                    found = table_ref[at + block // per_piece] * per_piece + block % per_piece
                    blocks.append(x_ref[jnp.where(k < count, found, empty)])
                adj = [adj_ref[side * per_side + i, k] for k in range(slots)]
                out_ref[i, j] = jnp.dot(
                    jnp.concatenate(adj, axis=1),
                    jnp.concatenate(blocks, axis=0),
                    preferred_element_type=F32,
                ).astype(out_ref.dtype)
            return carry

        lax.fori_loop(0, groups, some_rows, 0)


def spmm(meta, place, pieces, own, other):
    smem = pl.BlockSpec(memory_space=pltpu.SMEM)
    anywhere = pl.BlockSpec(memory_space=pl.ANY)
    blocks, bs, half = pieces[0].shape
    rows = own.shape[0] * CORE
    return pl.pallas_call(
        spmm_kernel,
        out_shape=jax.ShapeDtypeStruct((NCOL, CORE, bs, half), BF16),
        in_specs=[smem, smem, smem] + [anywhere] * (Y + 2),
        out_specs=pl.BlockSpec(memory_space=pltpu.VMEM),
        scratch_shapes=[
            pltpu.VMEM((blocks * Y + 1, bs, half), BF16),
            pltpu.VMEM((rows,) + own.shape[1:], BF16),
            pltpu.SemaphoreType.DMA((Y,)),
            pltpu.SemaphoreType.DMA((rows // 4,)),
        ],
        compiler_params=pltpu.CompilerParams(vmem_limit_bytes=60 * 1024 * 1024),
    )(meta, jnp.asarray(piece_table().reshape(-1)), place, *pieces, own, other)


def contract_rows(a, b):
    return lax.dot_general(a, b, (((0,), (0,)), ((), ())), preferred_element_type=F32)


def times_transpose(a, b):
    return lax.dot_general(a, b, (((1,), (1,)), ((), ())), preferred_element_type=F32)


def local(
    grad_out, mask_top, mask_mid, feats_in, feats_mid, weight_first, weight_second,
    adj_blocks, block_cols, block_counts,
):
    bs, feats = grad_out.shape
    half = feats // CORE
    core = lax.axis_index("core")
    nodes = bs * Y * ZL * CORE * X * ZH
    norm_scale = 1.0 / jnp.sqrt(F32(nodes))

    def my_half(v):
        return lax.dynamic_slice_in_dim(v, core * half, half, axis=v.ndim - 1)

    adj = adj_blocks[:, 0]
    meta = jnp.concatenate(
        [block_cols[:, 0], block_counts, jnp.zeros((NCOL, 16 - 13), jnp.int32)], axis=1
    )
    meta = lax.all_gather(meta, "core", axis=0, tiled=True).reshape(-1)
    place = jnp.stack([lax.axis_index("y"), core]).astype(jnp.int32)

    with jax.named_scope("pair_inputs"):
        grad_top = jnp.where(mask_top > 0, grad_out, jnp.zeros_like(grad_out))
        grad_top, meta = lax.optimization_barrier((grad_top, meta))
        unit_top = my_half(lax.all_gather(grad_top, "core", axis=0, tiled=True))
        pair = lax.all_gather(
            jnp.stack([mask_mid.astype(BF16), feats_mid, feats_in]), "core", axis=1, tiled=True
        )
        mask_pair = my_half(pair[0])
        feats_mid_pair = pair[1]
    with jax.named_scope("group_feats"):
        feats_in_group = everyone(pair[2], COLS, NCOL).reshape(-1, feats)

    def gather_z(unit):
        return everyone(unit, "zl", ZL).reshape(-1, bs, half)

    with jax.named_scope("section_top"):
        units = gather_z(unit_top)
        adj, units = lax.optimization_barrier((adj, units))
        other_adj = lax.ppermute(adj, "core", [(0, 1), (1, 0)])
        pieces, other_adj = gather_y(units, other_adj)
        partial_top = spmm(meta, place, pieces, adj, other_adj)
        parts = lax.all_to_all(
            partial_top.reshape(NCOL, CORE * bs, half), COLS, 0, 0, tiled=True
        )
        agg_top = jnp.sum(parts.astype(F32), axis=0).astype(BF16)
        agg_top_both = lax.all_gather(agg_top, "core", axis=1, tiled=True)
        term_second = contract_rows(feats_mid_pair, agg_top)
        weight_half = lax.dynamic_slice_in_dim(weight_second, core * half, half, axis=0)
        hidden = times_transpose(agg_top_both, weight_half)
        grad_mid = jnp.where(mask_pair > 0, hidden, jnp.zeros_like(hidden)).astype(BF16)
    with jax.named_scope("section_mid"):
        partial_mid = spmm(meta, place, gather_y(gather_z(grad_mid))[0], adj, other_adj)
        term_first = contract_rows(feats_in_group, partial_mid.reshape(-1, half))
        terms = jnp.stack([term_first, term_second]).astype(BF16)
        terms = terms.reshape(2, NCOL, feats // NCOL, half).transpose(1, 0, 2, 3)
        sent = jnp.concatenate(
            [partial_mid.reshape(NCOL, CORE * bs, half), terms.reshape(NCOL, -1, half)], axis=1
        )
        parts = lax.all_to_all(sent, COLS, 0, 0, tiled=True)
        summed = jnp.sum(parts.astype(F32), axis=0)
        agg_mid = summed[: CORE * bs].astype(BF16)
        own_nodes = lax.all_gather(agg_mid, "core", axis=1, tiled=True)
        own_nodes = lax.dynamic_slice_in_dim(own_nodes, core * bs, bs, axis=0)
        grad_in = times_transpose(own_nodes, weight_first).astype(BF16)
    with jax.named_scope("weight_sums"):
        piece = summed[CORE * bs :]
        over_y = everyone(piece.astype(BF16), "y", Y)
        piece = jnp.sum(over_y.reshape((Y,) + piece.shape).astype(F32), axis=0)
        over_xz = everyone(piece.astype(BF16), ("x", "zh", "zl"), NCOL * ZL)
        over_x = jnp.sum(over_xz.reshape((NCOL, ZL) + piece.shape).astype(F32), axis=1)
        over_x = over_x.reshape(NCOL, 2, feats // NCOL, half)
        whole = lax.all_gather(over_x * norm_scale, "core", axis=3, tiled=True)
        whole = whole.transpose(1, 0, 2, 3).reshape(2, feats, feats)
    return (grad_in, whole[0], whole[1])


def solution(mesh):
    parts = Mesh(mesh.devices.reshape(Y, ZL, CORE, X, ZH), AXES)
    nodes = P(AXES, None)
    return jax.shard_map(
        local,
        mesh=parts,
        in_specs=(
            nodes, nodes, nodes, nodes, nodes, P(), P(),
            P(ROWS, COLS, None, None, None),
            P(ROWS, COLS, None),
            P(ROWS, COLS),
        ),
        out_specs=(nodes, P(), P()),
        check_vma=False,
    )
```

```python
import jax
import jax.numpy as jnp
import numpy as np
from jax import lax
from jax.experimental import pallas as pl
from jax.experimental.pallas import tpu as pltpu
from jax.sharding import Mesh, PartitionSpec as P

Y, ZL, CORE, X, ZH = 8, 4, 2, 4, 2
AXES = ("y", "zl", "core", "x", "zh")
ROWS = ("y", "zl", "core")
COLS = ("x", "zh")
NCOL = X * ZH
BF16, F32 = jnp.bfloat16, jnp.float32
CHUNK, TOGETHER = 4, 8


def everyone(value, axes, count):
    return lax.all_to_all(
        jnp.broadcast_to(value[None], (count,) + value.shape), axes, 0, 0, tiled=True
    )


def y_pairs(which):
    pairs = []
    for y in range(Y):
        for core in range(CORE):
            up = (y + core + which) % 2 == 0
            pairs.append((y * CORE + core, (y + (1 if up else -1)) % Y * CORE + core))
    return pairs


def piece_table():
    step = [dict(y_pairs(0)), dict(y_pairs(1))]
    table = np.zeros((Y * CORE, Y), np.int32)
    for me in range(Y * CORE):
        for piece, hops in enumerate(
            ((), (0,), (1,), (1, 0), (0, 1), (0, 1, 0), (1, 0, 1), (1, 0, 1, 0))
        ):
            at = me
            for hop in hops:
                at = step[hop][at]
            table[me, at // CORE] = piece
    return table


def gather_y(mine, beside=None):
    def swap(value, which):
        return lax.ppermute(value, ("y", "core"), y_pairs(which))

    first, second = swap(mine, 0), swap(mine, 1)
    third, fourth = swap(first, 1), swap(second, 0)
    fifth, sixth = swap(third, 0), swap(fourth, 1)
    if beside is not None:
        fifth, beside = lax.optimization_barrier((fifth, beside))
    last = swap(fifth, 1)
    return (mine, first, second, third, fourth, fifth, sixth, last), beside


def spmm_kernel(meta_ref, table_ref, place_ref, *refs):
    pieces, refs = refs[:Y], refs[Y:]
    own_ref, other_ref, out_ref, x_ref, adj_ref, acc_ref, list_ref, x_sem, adj_sem = refs
    core = place_ref[1]
    at = (place_ref[0] * CORE + core) * Y
    per_side, slots = own_ref.shape[0], own_ref.shape[1]
    chunks = slots // CHUNK
    per_piece = pieces[0].shape[0]
    empty = x_ref.shape[0] - 1
    x_copies = [
        pltpu.make_async_copy(ref, x_ref.at[pl.ds(p * per_piece, per_piece)], x_sem.at[p])
        for p, ref in enumerate(pieces)
    ]
    for copy in x_copies:
        copy.start()

    def adj_copy(ref, i, c, item):
        return pltpu.make_async_copy(
            ref.at[i, pl.ds(c * CHUNK, CHUNK)], adj_ref.at[item], adj_sem.at[item]
        )

    total = jnp.int32(0)
    for side, ref in enumerate((own_ref, other_ref)):
        j = jnp.bitwise_xor(core, side)
        for i in range(per_side):
            count = meta_ref[(j * per_side + i) * 16 + slots]
            for c in range(chunks):
                live = count > c * CHUNK

                @pl.when(live)
                def _(ref=ref, i=i, c=c, side=side, total=total):
                    list_ref[total] = (side * per_side + i) * chunks + c
                    adj_copy(ref, i, c, total).start()

                total = total + live.astype(jnp.int32)

    acc_ref[...] = jnp.zeros(acc_ref.shape, acc_ref.dtype)
    x_ref[empty] = jnp.zeros(x_ref.shape[1:], x_ref.dtype)
    for copy in x_copies:
        copy.wait()

    def some_items(s, carry):
        for t in range(TOGETHER):
            item = s * TOGETHER + t

            @pl.when(item < total)
            def _(item=item):
                adj_copy(own_ref, 0, 0, item).wait()

        for t in range(TOGETHER):
            item = s * TOGETHER + t
            real = item < total
            item = jnp.where(real, item, 0)
            what = list_ref[item]
            row, c = what // chunks, what % chunks
            j = jnp.bitwise_xor(core, row // per_side)
            base = (j * per_side + row % per_side) * 16
            count = jnp.where(real, meta_ref[base + slots], 0)
            blocks = []
            for k in range(CHUNK):
                slot = c * CHUNK + k
                block = meta_ref[base + slot]
                found = table_ref[at + block // per_piece] * per_piece + block % per_piece
                blocks.append(x_ref[jnp.where(slot < count, found, empty)])
            acc_ref[row] += jnp.dot(
                jnp.concatenate([adj_ref[item, k] for k in range(CHUNK)], axis=1),
                jnp.concatenate(blocks, axis=0),
                preferred_element_type=F32,
            )
        return carry

    lax.fori_loop(0, (total + TOGETHER - 1) // TOGETHER, some_items, 0)
    for side in range(CORE):
        j = jnp.bitwise_xor(core, side)
        for i in range(per_side):
            out_ref[i, j] = acc_ref[side * per_side + i].astype(out_ref.dtype)


def spmm(meta, place, pieces, own, other):
    smem = pl.BlockSpec(memory_space=pltpu.SMEM)
    anywhere = pl.BlockSpec(memory_space=pl.ANY)
    blocks, bs, half = pieces[0].shape
    rows, slots = own.shape[0] * CORE, own.shape[1]
    items = rows * (slots // CHUNK)
    return pl.pallas_call(
        spmm_kernel,
        out_shape=jax.ShapeDtypeStruct((NCOL, CORE, bs, half), BF16),
        in_specs=[smem, smem, smem] + [anywhere] * (Y + 2),
        out_specs=pl.BlockSpec(memory_space=pltpu.VMEM),
        scratch_shapes=[
            pltpu.VMEM((blocks * Y + 1, bs, half), BF16),
            pltpu.VMEM((items, CHUNK, bs, bs), BF16),
            pltpu.VMEM((rows, bs, half), F32),
            pltpu.SMEM((items,), jnp.int32),
            pltpu.SemaphoreType.DMA((Y,)),
            pltpu.SemaphoreType.DMA((items,)),
        ],
        compiler_params=pltpu.CompilerParams(vmem_limit_bytes=60 * 1024 * 1024),
    )(meta, jnp.asarray(piece_table().reshape(-1)), place, *pieces, own, other)


def contract_rows(a, b):
    return lax.dot_general(a, b, (((0,), (0,)), ((), ())), preferred_element_type=F32)


def times_transpose(a, b):
    return lax.dot_general(a, b, (((1,), (1,)), ((), ())), preferred_element_type=F32)


def local(
    grad_out, mask_top, mask_mid, feats_in, feats_mid, weight_first, weight_second,
    adj_blocks, block_cols, block_counts,
):
    bs, feats = grad_out.shape
    half = feats // CORE
    core = lax.axis_index("core")
    nodes = bs * Y * ZL * CORE * X * ZH
    norm_scale = 1.0 / jnp.sqrt(F32(nodes))

    def my_half(v):
        return lax.dynamic_slice_in_dim(v, core * half, half, axis=v.ndim - 1)

    adj = adj_blocks[:, 0]
    place = jnp.stack([lax.axis_index("y"), core]).astype(jnp.int32)

    with jax.named_scope("pair_inputs"):
        grad_top = jnp.where(mask_top > 0, grad_out, jnp.zeros_like(grad_out))
        meta = jnp.concatenate([block_cols[:, 0], block_counts], axis=1).astype(BF16)
        meta = jnp.pad(meta, ((0, 16 - meta.shape[0]), (0, feats - meta.shape[1])))
        joined = lax.all_gather(jnp.concatenate([grad_top, meta], axis=0), "core", axis=0)
        unit_top = my_half(joined[:, :bs]).reshape(CORE * bs, half)
        meta = joined[:, bs : bs + NCOL, :16].astype(jnp.int32).reshape(-1)
        unit_top, adj = lax.optimization_barrier((unit_top, adj))
        other_adj = lax.ppermute(adj, "core", [(0, 1), (1, 0)])
        pair = lax.all_gather(
            jnp.stack([mask_mid.astype(BF16), feats_mid, feats_in]), "core", axis=1, tiled=True
        )
        mask_pair = my_half(pair[0])
        feats_mid_pair = pair[1]
    with jax.named_scope("group_feats"):
        feats_in_group = everyone(pair[2], COLS, NCOL).reshape(-1, feats)

    def gather_z(unit):
        return everyone(unit, "zl", ZL).reshape(-1, bs, half)

    with jax.named_scope("section_top"):
        pieces, other_adj = gather_y(gather_z(unit_top), other_adj)
        partial_top = spmm(meta, place, pieces, adj, other_adj)
        parts = lax.all_to_all(
            partial_top.reshape(NCOL, CORE * bs, half), COLS, 0, 0, tiled=True
        )
        agg_top = jnp.sum(parts.astype(F32), axis=0).astype(BF16)
        agg_top_both = lax.all_gather(agg_top, "core", axis=1, tiled=True)
        term_second = contract_rows(feats_mid_pair, agg_top)
        weight_half = lax.dynamic_slice_in_dim(weight_second, core * half, half, axis=0)
        hidden = times_transpose(agg_top_both, weight_half)
        grad_mid = jnp.where(mask_pair > 0, hidden, jnp.zeros_like(hidden)).astype(BF16)
    with jax.named_scope("section_mid"):
        partial_mid = spmm(meta, place, gather_y(gather_z(grad_mid))[0], adj, other_adj)
        term_first = contract_rows(feats_in_group, partial_mid.reshape(-1, half))
        terms = jnp.stack([term_first, term_second]).astype(BF16)
        terms = terms.reshape(2, NCOL, feats // NCOL, half).transpose(1, 0, 2, 3)
        sent = jnp.concatenate(
            [partial_mid.reshape(NCOL, CORE * bs, half), terms.reshape(NCOL, -1, half)], axis=1
        )
        parts = lax.all_to_all(sent, COLS, 0, 0, tiled=True)
        summed = jnp.sum(parts.astype(F32), axis=0)
        agg_mid = summed[: CORE * bs].astype(BF16)
        own_nodes = lax.all_gather(agg_mid, "core", axis=1, tiled=True)
        own_nodes = lax.dynamic_slice_in_dim(own_nodes, core * bs, bs, axis=0)
        grad_in = times_transpose(own_nodes, weight_first).astype(BF16)
    with jax.named_scope("weight_sums"):
        piece = summed[CORE * bs :]
        over_y = everyone(piece.astype(BF16), "y", Y)
        piece = jnp.sum(over_y.reshape((Y,) + piece.shape).astype(F32), axis=0)
        over_xz = everyone(piece.astype(BF16), ("x", "zh", "zl"), NCOL * ZL)
        over_x = jnp.sum(over_xz.reshape((NCOL, ZL) + piece.shape).astype(F32), axis=1)
        over_x = over_x.reshape(NCOL, 2, feats // NCOL, half)
        whole = lax.all_gather(over_x * norm_scale, "core", axis=3, tiled=True)
        whole = whole.transpose(1, 0, 2, 3).reshape(2, feats, feats)
    return (grad_in, whole[0], whole[1])


def solution(mesh):
    parts = Mesh(mesh.devices.reshape(Y, ZL, CORE, X, ZH), AXES)
    nodes = P(AXES, None)
    return jax.shard_map(
        local,
        mesh=parts,
        in_specs=(
            nodes, nodes, nodes, nodes, nodes, P(), P(),
            P(ROWS, COLS, None, None, None),
            P(ROWS, COLS, None),
            P(ROWS, COLS),
        ),
        out_specs=(nodes, P(), P()),
        check_vma=False,
    )
```

```python
import jax
import jax.numpy as jnp
import numpy as np
from jax import lax
from jax.experimental import pallas as pl
from jax.experimental.pallas import tpu as pltpu
from jax.sharding import Mesh, PartitionSpec as P

Y, ZL, CORE, X, ZH = 8, 4, 2, 4, 2
AXES = ("y", "zl", "core", "x", "zh")
ROWS = ("y", "zl", "core")
COLS = ("x", "zh")
NCOL = X * ZH
BF16, F32 = jnp.bfloat16, jnp.float32


def everyone(value, axes, count):
    return lax.all_to_all(
        jnp.broadcast_to(value[None], (count,) + value.shape), axes, 0, 0, tiled=True
    )


def y_pairs(which):
    pairs = []
    for y in range(Y):
        for core in range(CORE):
            up = (y + core + which) % 2 == 0
            pairs.append((y * CORE + core, (y + (1 if up else -1)) % Y * CORE + core))
    return pairs


def piece_table():
    step = [dict(y_pairs(0)), dict(y_pairs(1))]
    table = np.zeros((Y * CORE, Y), np.int32)
    for me in range(Y * CORE):
        for piece, hops in enumerate(
            ((), (0,), (1,), (1, 0), (0, 1), (0, 1, 0), (1, 0, 1), (1, 0, 1, 0))
        ):
            at = me
            for hop in hops:
                at = step[hop][at]
            table[me, at // CORE] = piece
    return table


def gather_y(mine, beside=None, run=None):
    def swap(value, which):
        return lax.ppermute(value, ("y", "core"), y_pairs(which))

    first, second = swap(mine, 0), swap(mine, 1)
    if run is not None:
        first, second, beside = lax.optimization_barrier((first, second, beside))
        beside = run(beside)
    third, fourth = swap(first, 1), swap(second, 0)
    if run is not None:
        third, fourth, beside = lax.optimization_barrier((third, fourth, beside))
    fifth, sixth = swap(third, 0), swap(fourth, 1)
    opposite = lax.ppermute(mine, "y", [(y, (y + Y // 2) % Y) for y in range(Y)])
    return (mine, first, second, third, fourth, fifth, sixth, opposite), beside


def spmm_kernel(meta_ref, table_ref, place_ref, *refs):
    pieces, (own_ref, other_ref, out_ref, x_ref, adj_ref, x_sem, adj_sem) = refs[:Y], refs[Y:]
    core = place_ref[1]
    at = (place_ref[0] * CORE + core) * Y
    per_side, slots = own_ref.shape[0], own_ref.shape[1]
    per_piece = pieces[0].shape[0]
    together = 4
    groups = per_side // together
    empty = x_ref.shape[0] - 1
    x_copies = [
        pltpu.make_async_copy(ref, x_ref.at[pl.ds(p * per_piece, per_piece)], x_sem.at[p])
        for p, ref in enumerate(pieces)
    ]

    def adj_copy(ref, side, m):
        return pltpu.make_async_copy(
            ref.at[pl.ds(m * together, together)],
            adj_ref.at[pl.ds(side * per_side + m * together, together)],
            adj_sem.at[side * groups + m],
        )

    for copy in x_copies:
        copy.start()
    for side, ref in enumerate((own_ref, other_ref)):
        for m in range(groups):
            adj_copy(ref, side, m).start()
    x_ref[empty] = jnp.zeros(x_ref.shape[1:], x_ref.dtype)
    for copy in x_copies:
        copy.wait()

    for side, ref in enumerate((own_ref, other_ref)):
        j = jnp.bitwise_xor(core, side)

        def some_rows(m, carry, side=side, ref=ref, j=j):
            adj_copy(ref, side, m).wait()
            for t in range(together):
                i = m * together + t
                base = (j * per_side + i) * 16
                count = meta_ref[base + slots]
                blocks = []
                for k in range(slots):
                    block = meta_ref[base + k]
                    found = table_ref[at + block // per_piece] * per_piece + block % per_piece
                    blocks.append(x_ref[jnp.where(k < count, found, empty)])
                adj = [adj_ref[side * per_side + i, k] for k in range(slots)]
                out_ref[i, j] = jnp.dot(
                    jnp.concatenate(adj, axis=1),
                    jnp.concatenate(blocks, axis=0),
                    preferred_element_type=F32,
                ).astype(out_ref.dtype)
            return carry

        lax.fori_loop(0, groups, some_rows, 0)


def spmm(meta, place, pieces, own, other):
    smem = pl.BlockSpec(memory_space=pltpu.SMEM)
    anywhere = pl.BlockSpec(memory_space=pl.ANY)
    blocks, bs, half = pieces[0].shape
    rows = own.shape[0] * CORE
    return pl.pallas_call(
        spmm_kernel,
        out_shape=jax.ShapeDtypeStruct((NCOL, CORE, bs, half), BF16),
        in_specs=[smem, smem, smem] + [anywhere] * (Y + 2),
        out_specs=pl.BlockSpec(memory_space=pltpu.VMEM),
        scratch_shapes=[
            pltpu.VMEM((blocks * Y + 1, bs, half), BF16),
            pltpu.VMEM((rows,) + own.shape[1:], BF16),
            pltpu.SemaphoreType.DMA((Y,)),
            pltpu.SemaphoreType.DMA((rows // 4,)),
        ],
        compiler_params=pltpu.CompilerParams(vmem_limit_bytes=60 * 1024 * 1024),
    )(meta, jnp.asarray(piece_table().reshape(-1)), place, *pieces, own, other)


def contract_rows(a, b):
    return lax.dot_general(a, b, (((0,), (0,)), ((), ())), preferred_element_type=F32)


def times_transpose(a, b):
    return lax.dot_general(a, b, (((1,), (1,)), ((), ())), preferred_element_type=F32)


def local(
    grad_out, mask_top, mask_mid, feats_in, feats_mid, weight_first, weight_second,
    adj_blocks, block_cols, block_counts,
):
    bs, feats = grad_out.shape
    half = feats // CORE
    core = lax.axis_index("core")
    nodes = bs * Y * ZL * CORE * X * ZH
    norm_scale = 1.0 / jnp.sqrt(F32(nodes))

    def my_half(v):
        return lax.dynamic_slice_in_dim(v, core * half, half, axis=v.ndim - 1)

    adj = adj_blocks[:, 0]
    meta = jnp.concatenate(
        [block_cols[:, 0], block_counts, jnp.zeros((NCOL, 16 - 13), jnp.int32)], axis=1
    )
    place = jnp.stack([lax.axis_index("y"), core]).astype(jnp.int32)

    with jax.named_scope("pair_inputs"):
        grad_top = jnp.where(mask_top > 0, grad_out, jnp.zeros_like(grad_out))
        unit_top = my_half(lax.all_gather(grad_top, "core", axis=0, tiled=True))
        pair = lax.all_gather(
            jnp.stack([mask_mid.astype(BF16), feats_mid, feats_in]), "core", axis=1, tiled=True
        )
        mask_pair = my_half(pair[0])
        feats_mid_pair = pair[1]

    def pair_blocks(blocks):
        adj, meta = blocks
        meta = lax.all_gather(meta, "core", axis=0, tiled=True).reshape(-1)
        return lax.ppermute(adj, "core", [(0, 1), (1, 0)]), meta

    with jax.named_scope("group_feats"):
        feats_in_group = everyone(pair[2], COLS, NCOL).reshape(-1, feats)

    def gather_z(unit):
        return everyone(unit, "zl", ZL).reshape(-1, bs, half)

    with jax.named_scope("section_top"):
        pieces, (other_adj, meta) = gather_y(gather_z(unit_top), (adj, meta), pair_blocks)
        partial_top = spmm(meta, place, pieces, adj, other_adj)
        parts = lax.all_to_all(
            partial_top.reshape(NCOL, CORE * bs, half), COLS, 0, 0, tiled=True
        )
        agg_top = jnp.sum(parts.astype(F32), axis=0).astype(BF16)
        agg_top_both = lax.all_gather(agg_top, "core", axis=1, tiled=True)
        term_second = contract_rows(feats_mid_pair, agg_top)
        weight_half = lax.dynamic_slice_in_dim(weight_second, core * half, half, axis=0)
        hidden = times_transpose(agg_top_both, weight_half)
        grad_mid = jnp.where(mask_pair > 0, hidden, jnp.zeros_like(hidden)).astype(BF16)
    with jax.named_scope("section_mid"):
        pieces, _ = gather_y(gather_z(grad_mid))
        partial_mid = spmm(meta, place, pieces, adj, other_adj)
        term_first = contract_rows(feats_in_group, partial_mid.reshape(-1, half))
        terms = jnp.stack([term_first, term_second]).astype(BF16)
        terms = terms.reshape(2, NCOL, feats // NCOL, half).transpose(1, 0, 2, 3)
        sent = jnp.concatenate(
            [partial_mid.reshape(NCOL, CORE * bs, half), terms.reshape(NCOL, -1, half)], axis=1
        )
        parts = lax.all_to_all(sent, COLS, 0, 0, tiled=True)
        summed = jnp.sum(parts.astype(F32), axis=0)
        agg_mid = summed[: CORE * bs].astype(BF16)
        own_nodes = lax.all_gather(agg_mid, "core", axis=1, tiled=True)
        own_nodes = lax.dynamic_slice_in_dim(own_nodes, core * bs, bs, axis=0)
        grad_in = times_transpose(own_nodes, weight_first).astype(BF16)
    with jax.named_scope("weight_sums"):
        piece = summed[CORE * bs :]
        over_y = everyone(piece.astype(BF16), "y", Y)
        piece = jnp.sum(over_y.reshape((Y,) + piece.shape).astype(F32), axis=0)
        over_xz = everyone(piece.astype(BF16), ("x", "zh", "zl"), NCOL * ZL)
        over_x = jnp.sum(over_xz.reshape((NCOL, ZL) + piece.shape).astype(F32), axis=1)
        over_x = over_x.reshape(NCOL, 2, feats // NCOL, half)
        whole = lax.all_gather(over_x * norm_scale, "core", axis=3, tiled=True)
        whole = whole.transpose(1, 0, 2, 3).reshape(2, feats, feats)
    return (grad_in, whole[0], whole[1])


def solution(mesh):
    parts = Mesh(mesh.devices.reshape(Y, ZL, CORE, X, ZH), AXES)
    nodes = P(AXES, None)
    return jax.shard_map(
        local,
        mesh=parts,
        in_specs=(
            nodes, nodes, nodes, nodes, nodes, P(), P(),
            P(ROWS, COLS, None, None, None),
            P(ROWS, COLS, None),
            P(ROWS, COLS),
        ),
        out_specs=(nodes, P(), P()),
        check_vma=False,
    )
```

```python
import jax
import jax.numpy as jnp
import numpy as np
from jax import lax
from jax.experimental import pallas as pl
from jax.experimental.pallas import tpu as pltpu
from jax.sharding import Mesh, PartitionSpec as P

Y, ZL, CORE, X, ZH = 8, 4, 2, 4, 2
AXES = ("y", "zl", "core", "x", "zh")
ROWS = ("y", "zl", "core")
COLS = ("x", "zh")
NCOL = X * ZH
BF16, F32 = jnp.bfloat16, jnp.float32


def everyone(value, axes, count):
    return lax.all_to_all(
        jnp.broadcast_to(value[None], (count,) + value.shape), axes, 0, 0, tiled=True
    )


def y_pairs(which):
    pairs = []
    for y in range(Y):
        for core in range(CORE):
            up = (y + core + which) % 2 == 0
            pairs.append((y * CORE + core, (y + (1 if up else -1)) % Y * CORE + core))
    return pairs


def piece_table():
    step = [dict(y_pairs(0)), dict(y_pairs(1))]
    table = np.zeros((Y * CORE, Y), np.int32)
    for me in range(Y * CORE):
        for piece, hops in enumerate(
            ((), (0,), (1,), (1, 0), (0, 1), (0, 1, 0), (1, 0, 1), (1, 0, 1, 0))
        ):
            at = me
            for hop in hops:
                at = step[hop][at]
            table[me, at // CORE] = piece
    return table


def gather_y(mine, early=None, late=None):
    def swap(value, which):
        return lax.ppermute(value, ("y", "core"), y_pairs(which))

    first, second = swap(mine, 0), swap(mine, 1)
    third, fourth = swap(first, 1), swap(second, 0)
    if early is not None:
        third, early = lax.optimization_barrier((third, early))
    fifth, sixth = swap(third, 0), swap(fourth, 1)
    if late is not None:
        fifth, late = lax.optimization_barrier((fifth, late))
    last = swap(fifth, 1)
    return (mine, first, second, third, fourth, fifth, sixth, last), early, late


def spmm_kernel(meta_ref, table_ref, place_ref, *refs):
    pieces, (own_ref, other_ref, out_ref, x_ref, adj_ref, x_sem, adj_sem) = refs[:Y], refs[Y:]
    core = place_ref[1]
    at = (place_ref[0] * CORE + core) * Y
    per_side, slots = own_ref.shape[0], own_ref.shape[1]
    per_piece = pieces[0].shape[0]
    together = 4
    groups = per_side // together
    empty = x_ref.shape[0] - 1
    x_copies = [
        pltpu.make_async_copy(ref, x_ref.at[pl.ds(p * per_piece, per_piece)], x_sem.at[p])
        for p, ref in enumerate(pieces)
    ]

    def adj_copy(ref, side, m):
        return pltpu.make_async_copy(
            ref.at[pl.ds(m * together, together)],
            adj_ref.at[pl.ds(side * per_side + m * together, together)],
            adj_sem.at[side * groups + m],
        )

    for copy in x_copies:
        copy.start()
    for side, ref in enumerate((own_ref, other_ref)):
        for m in range(groups):
            adj_copy(ref, side, m).start()
    x_ref[empty] = jnp.zeros(x_ref.shape[1:], x_ref.dtype)
    for copy in x_copies:
        copy.wait()

    for side, ref in enumerate((own_ref, other_ref)):
        j = jnp.bitwise_xor(core, side)

        def some_rows(m, carry, side=side, ref=ref, j=j):
            adj_copy(ref, side, m).wait()
            for t in range(together):
                i = m * together + t
                base = (j * per_side + i) * 16
                count = meta_ref[base + slots]
                blocks = []
                for k in range(slots):
                    block = meta_ref[base + k]
                    found = table_ref[at + block // per_piece] * per_piece + block % per_piece
                    blocks.append(x_ref[jnp.where(k < count, found, empty)])
                adj = [adj_ref[side * per_side + i, k] for k in range(slots)]
                out_ref[i, j] = jnp.dot(
                    jnp.concatenate(adj, axis=1),
                    jnp.concatenate(blocks, axis=0),
                    preferred_element_type=F32,
                ).astype(out_ref.dtype)
            return carry

        lax.fori_loop(0, groups, some_rows, 0)


def spmm(meta, place, pieces, own, other):
    smem = pl.BlockSpec(memory_space=pltpu.SMEM)
    anywhere = pl.BlockSpec(memory_space=pl.ANY)
    blocks, bs, half = pieces[0].shape
    rows = own.shape[0] * CORE
    return pl.pallas_call(
        spmm_kernel,
        out_shape=jax.ShapeDtypeStruct((NCOL, CORE, bs, half), BF16),
        in_specs=[smem, smem, smem] + [anywhere] * (Y + 2),
        out_specs=pl.BlockSpec(memory_space=pltpu.VMEM),
        scratch_shapes=[
            pltpu.VMEM((blocks * Y + 1, bs, half), BF16),
            pltpu.VMEM((rows,) + own.shape[1:], BF16),
            pltpu.SemaphoreType.DMA((Y,)),
            pltpu.SemaphoreType.DMA((rows // 4,)),
        ],
        compiler_params=pltpu.CompilerParams(vmem_limit_bytes=60 * 1024 * 1024),
    )(meta, jnp.asarray(piece_table().reshape(-1)), place, *pieces, own, other)


def contract_rows(a, b):
    return lax.dot_general(a, b, (((0,), (0,)), ((), ())), preferred_element_type=F32)


def times_transpose(a, b):
    return lax.dot_general(a, b, (((1,), (1,)), ((), ())), preferred_element_type=F32)


def local(
    grad_out, mask_top, mask_mid, feats_in, feats_mid, weight_first, weight_second,
    adj_blocks, block_cols, block_counts,
):
    bs, feats = grad_out.shape
    half = feats // CORE
    core = lax.axis_index("core")
    nodes = bs * Y * ZL * CORE * X * ZH
    norm_scale = 1.0 / jnp.sqrt(F32(nodes))

    def my_half(v):
        return lax.dynamic_slice_in_dim(v, core * half, half, axis=v.ndim - 1)

    adj = adj_blocks[:, 0]
    meta = jnp.concatenate(
        [block_cols[:, 0], block_counts, jnp.zeros((NCOL, 16 - 13), jnp.int32)], axis=1
    )
    meta = lax.all_gather(meta, "core", axis=0, tiled=True).reshape(-1)
    place = jnp.stack([lax.axis_index("y"), core]).astype(jnp.int32)

    with jax.named_scope("pair_inputs"):
        grad_top = jnp.where(mask_top > 0, grad_out, jnp.zeros_like(grad_out))
        unit_top = my_half(lax.all_gather(grad_top, "core", axis=0, tiled=True))
        pair = lax.all_gather(
            jnp.stack([mask_mid.astype(BF16), feats_mid]), "core", axis=1, tiled=True
        )
        mask_pair = my_half(pair[0])
        feats_mid_pair = pair[1]
    def gather_z(unit):
        return everyone(unit, "zl", ZL).reshape(-1, bs, half)

    with jax.named_scope("section_top"):
        units = gather_z(unit_top)
        feats_in_pair = lax.all_gather(feats_in, "core", axis=0, tiled=True)
        adj, feats_in_pair, units = lax.optimization_barrier((adj, feats_in_pair, units))
        other_adj = lax.ppermute(adj, "core", [(0, 1), (1, 0)])
        feats_in_group = everyone(feats_in_pair, COLS, NCOL).reshape(-1, feats)
        pieces, meta, (other_adj, feats_in_group) = gather_y(
            units, meta, (other_adj, feats_in_group)
        )
        partial_top = spmm(meta, place, pieces, adj, other_adj)
        parts = lax.all_to_all(
            partial_top.reshape(NCOL, CORE * bs, half), COLS, 0, 0, tiled=True
        )
        agg_top = jnp.sum(parts.astype(F32), axis=0).astype(BF16)
        agg_top_both = lax.all_gather(agg_top, "core", axis=1, tiled=True)
        term_second = contract_rows(feats_mid_pair, agg_top)
        weight_half = lax.dynamic_slice_in_dim(weight_second, core * half, half, axis=0)
        hidden = times_transpose(agg_top_both, weight_half)
        grad_mid = jnp.where(mask_pair > 0, hidden, jnp.zeros_like(hidden)).astype(BF16)
    with jax.named_scope("section_mid"):
        partial_mid = spmm(meta, place, gather_y(gather_z(grad_mid))[0], adj, other_adj)
        term_first = contract_rows(feats_in_group, partial_mid.reshape(-1, half))
        terms = jnp.stack([term_first, term_second]).astype(BF16)
        terms = terms.reshape(2, NCOL, feats // NCOL, half).transpose(1, 0, 2, 3)
        sent = jnp.concatenate(
            [partial_mid.reshape(NCOL, CORE * bs, half), terms.reshape(NCOL, -1, half)], axis=1
        )
        parts = lax.all_to_all(sent, COLS, 0, 0, tiled=True)
        summed = jnp.sum(parts.astype(F32), axis=0)
        agg_mid = summed[: CORE * bs].astype(BF16)
        own_nodes = lax.all_gather(agg_mid, "core", axis=1, tiled=True)
        own_nodes = lax.dynamic_slice_in_dim(own_nodes, core * bs, bs, axis=0)
        grad_in = times_transpose(own_nodes, weight_first).astype(BF16)
    with jax.named_scope("weight_sums"):
        piece = summed[CORE * bs :]
        over_y = everyone(piece.astype(BF16), "y", Y)
        piece = jnp.sum(over_y.reshape((Y,) + piece.shape).astype(F32), axis=0)
        over_xz = everyone(piece.astype(BF16), ("x", "zh", "zl"), NCOL * ZL)
        over_x = jnp.sum(over_xz.reshape((NCOL, ZL) + piece.shape).astype(F32), axis=1)
        over_x = over_x.reshape(NCOL, 2, feats // NCOL, half)
        whole = lax.all_gather(over_x * norm_scale, "core", axis=3, tiled=True)
        whole = whole.transpose(1, 0, 2, 3).reshape(2, feats, feats)
    return (grad_in, whole[0], whole[1])


def solution(mesh):
    parts = Mesh(mesh.devices.reshape(Y, ZL, CORE, X, ZH), AXES)
    nodes = P(AXES, None)
    return jax.shard_map(
        local,
        mesh=parts,
        in_specs=(
            nodes, nodes, nodes, nodes, nodes, P(), P(),
            P(ROWS, COLS, None, None, None),
            P(ROWS, COLS, None),
            P(ROWS, COLS),
        ),
        out_specs=(nodes, P(), P()),
        check_vma=False,
    )
```

```python
import jax
import jax.numpy as jnp
import numpy as np
from jax import lax
from jax.experimental import pallas as pl
from jax.experimental.pallas import tpu as pltpu
from jax.sharding import Mesh, PartitionSpec as P

Y, ZL, CORE, X, ZH = 8, 4, 2, 4, 2
AXES = ("y", "zl", "core", "x", "zh")
ROWS = ("y", "zl", "core")
COLS = ("x", "zh")
NCOL = X * ZH
BF16, F32 = jnp.bfloat16, jnp.float32


def everyone(value, axes, count):
    return lax.all_to_all(
        jnp.broadcast_to(value[None], (count,) + value.shape), axes, 0, 0, tiled=True
    )


def y_pairs(which):
    pairs = []
    for y in range(Y):
        for core in range(CORE):
            up = (y + core + which) % 2 == 0
            pairs.append((y * CORE + core, (y + (1 if up else -1)) % Y * CORE + core))
    return pairs


def piece_table():
    step = [dict(y_pairs(0)), dict(y_pairs(1))]
    table = np.zeros((Y * CORE, Y), np.int32)
    for me in range(Y * CORE):
        for piece, hops in enumerate(
            ((), (0,), (1,), (1, 0), (0, 1), (0, 1, 0), (1, 0, 1), (1, 0, 1, 0))
        ):
            at = me
            for hop in hops:
                at = step[hop][at]
            table[me, at // CORE] = piece
    return table


def gather_y(mine, early=None, late=None):
    def swap(value, which):
        return lax.ppermute(value, ("y", "core"), y_pairs(which))

    first, second = swap(mine, 0), swap(mine, 1)
    third, fourth = swap(first, 1), swap(second, 0)
    if early is not None:
        third, early = lax.optimization_barrier((third, early))
    fifth, sixth = swap(third, 0), swap(fourth, 1)
    if late is not None:
        fifth, late = lax.optimization_barrier((fifth, late))
    last = swap(fifth, 1)
    return (mine, first, second, third, fourth, fifth, sixth, last), early, late


def spmm_kernel(meta_ref, table_ref, place_ref, *refs):
    pieces, (own_ref, other_ref, out_ref, x_ref, adj_ref, x_sem, adj_sem) = refs[:Y], refs[Y:]
    core = place_ref[1]
    at = (place_ref[0] * CORE + core) * Y
    per_side, slots = own_ref.shape[0], own_ref.shape[1]
    per_piece = pieces[0].shape[0]
    together = 4
    groups = per_side // together
    empty = x_ref.shape[0] - 1
    x_copies = [
        pltpu.make_async_copy(ref, x_ref.at[pl.ds(p * per_piece, per_piece)], x_sem.at[p])
        for p, ref in enumerate(pieces)
    ]

    def adj_copy(ref, side, m):
        return pltpu.make_async_copy(
            ref.at[pl.ds(m * together, together)],
            adj_ref.at[pl.ds(side * per_side + m * together, together)],
            adj_sem.at[side * groups + m],
        )

    for copy in x_copies:
        copy.start()
    for side, ref in enumerate((own_ref, other_ref)):
        for m in range(groups):
            adj_copy(ref, side, m).start()
    x_ref[empty] = jnp.zeros(x_ref.shape[1:], x_ref.dtype)
    for copy in x_copies:
        copy.wait()

    for side, ref in enumerate((own_ref, other_ref)):
        j = jnp.bitwise_xor(core, side)

        def some_rows(m, carry, side=side, ref=ref, j=j):
            adj_copy(ref, side, m).wait()
            for t in range(together):
                i = m * together + t
                base = (j * per_side + i) * 16
                count = meta_ref[base + slots]
                blocks = []
                for k in range(slots):
                    block = meta_ref[base + k]
                    found = table_ref[at + block // per_piece] * per_piece + block % per_piece
                    blocks.append(x_ref[jnp.where(k < count, found, empty)])
                adj = [adj_ref[side * per_side + i, k] for k in range(slots)]
                out_ref[i, j] = jnp.dot(
                    jnp.concatenate(adj, axis=1),
                    jnp.concatenate(blocks, axis=0),
                    preferred_element_type=F32,
                ).astype(out_ref.dtype)
            return carry

        lax.fori_loop(0, groups, some_rows, 0)


def spmm(meta, place, pieces, own, other):
    smem = pl.BlockSpec(memory_space=pltpu.SMEM)
    anywhere = pl.BlockSpec(memory_space=pl.ANY)
    blocks, bs, half = pieces[0].shape
    rows = own.shape[0] * CORE
    return pl.pallas_call(
        spmm_kernel,
        out_shape=jax.ShapeDtypeStruct((NCOL, CORE, bs, half), BF16),
        in_specs=[smem, smem, smem] + [anywhere] * (Y + 2),
        out_specs=pl.BlockSpec(memory_space=pltpu.VMEM),
        scratch_shapes=[
            pltpu.VMEM((blocks * Y + 1, bs, half), BF16),
            pltpu.VMEM((rows,) + own.shape[1:], BF16),
            pltpu.SemaphoreType.DMA((Y,)),
            pltpu.SemaphoreType.DMA((rows // 4,)),
        ],
        compiler_params=pltpu.CompilerParams(vmem_limit_bytes=60 * 1024 * 1024),
    )(meta, jnp.asarray(piece_table().reshape(-1)), place, *pieces, own, other)


def contract_rows(a, b):
    return lax.dot_general(a, b, (((0,), (0,)), ((), ())), preferred_element_type=F32)


def times_transpose(a, b):
    return lax.dot_general(a, b, (((1,), (1,)), ((), ())), preferred_element_type=F32)


def local(
    grad_out, mask_top, mask_mid, feats_in, feats_mid, weight_first, weight_second,
    adj_blocks, block_cols, block_counts,
):
    bs, feats = grad_out.shape
    half = feats // CORE
    core = lax.axis_index("core")
    nodes = bs * Y * ZL * CORE * X * ZH
    norm_scale = 1.0 / jnp.sqrt(F32(nodes))

    def my_half(v):
        return lax.dynamic_slice_in_dim(v, core * half, half, axis=v.ndim - 1)

    adj = adj_blocks[:, 0]
    meta = jnp.concatenate(
        [block_cols[:, 0], block_counts, jnp.zeros((NCOL, 16 - 13), jnp.int32)], axis=1
    )
    meta = lax.all_gather(meta, "core", axis=0, tiled=True).reshape(-1)
    place = jnp.stack([lax.axis_index("y"), core]).astype(jnp.int32)

    with jax.named_scope("pair_inputs"):
        grad_top = jnp.where(mask_top > 0, grad_out, jnp.zeros_like(grad_out))
        unit_top = my_half(lax.all_gather(grad_top, "core", axis=0, tiled=True))
        pair = lax.all_gather(
            jnp.stack([mask_mid.astype(BF16), feats_mid, feats_in]), "core", axis=1, tiled=True
        )
        mask_pair = my_half(pair[0])
        feats_mid_pair = pair[1]
    def gather_z(unit):
        return everyone(unit, "zl", ZL).reshape(-1, bs, half)

    with jax.named_scope("section_top"):
        units = gather_z(unit_top)
        adj, units = lax.optimization_barrier((adj, units))
        other_adj = lax.ppermute(adj, "core", [(0, 1), (1, 0)])
        pieces, meta, other_adj = gather_y(units, meta, other_adj)
        partial_top = spmm(meta, place, pieces, adj, other_adj)
        parts = lax.all_to_all(
            partial_top.reshape(NCOL, CORE * bs, half), COLS, 0, 0, tiled=True
        )
        agg_top = jnp.sum(parts.astype(F32), axis=0).astype(BF16)
        agg_top_both = lax.all_gather(agg_top, "core", axis=1, tiled=True)
        term_second = contract_rows(feats_mid_pair, agg_top)
        weight_half = lax.dynamic_slice_in_dim(weight_second, core * half, half, axis=0)
        hidden = times_transpose(agg_top_both, weight_half)
        grad_mid = jnp.where(mask_pair > 0, hidden, jnp.zeros_like(hidden)).astype(BF16)
    with jax.named_scope("section_mid"):
        mine = pair[2]
        other = lax.ppermute(mine, "zh", [(0, 1), (1, 0)])
        units = gather_z(grad_mid)
        first_zh = lax.axis_index("zh") == 0
        both = jnp.stack([jnp.where(first_zh, mine, other), jnp.where(first_zh, other, mine)])
        feats_in_group = everyone(both, "x", X).reshape(-1, feats)
        partial_mid = spmm(meta, place, gather_y(units)[0], adj, other_adj)
        term_first = contract_rows(feats_in_group, partial_mid.reshape(-1, half))
        terms = jnp.stack([term_first, term_second]).astype(BF16)
        terms = terms.reshape(2, NCOL, feats // NCOL, half).transpose(1, 0, 2, 3)
        sent = jnp.concatenate(
            [partial_mid.reshape(NCOL, CORE * bs, half), terms.reshape(NCOL, -1, half)], axis=1
        )
        parts = lax.all_to_all(sent, COLS, 0, 0, tiled=True)
        summed = jnp.sum(parts.astype(F32), axis=0)
        agg_mid = summed[: CORE * bs].astype(BF16)
        own_nodes = lax.all_gather(agg_mid, "core", axis=1, tiled=True)
        own_nodes = lax.dynamic_slice_in_dim(own_nodes, core * bs, bs, axis=0)
        grad_in = times_transpose(own_nodes, weight_first).astype(BF16)
    with jax.named_scope("weight_sums"):
        piece = summed[CORE * bs :]
        over_y = everyone(piece.astype(BF16), "y", Y)
        piece = jnp.sum(over_y.reshape((Y,) + piece.shape).astype(F32), axis=0)
        over_xz = everyone(piece.astype(BF16), ("x", "zh", "zl"), NCOL * ZL)
        over_x = jnp.sum(over_xz.reshape((NCOL, ZL) + piece.shape).astype(F32), axis=1)
        over_x = over_x.reshape(NCOL, 2, feats // NCOL, half)
        whole = lax.all_gather(over_x * norm_scale, "core", axis=3, tiled=True)
        whole = whole.transpose(1, 0, 2, 3).reshape(2, feats, feats)
    return (grad_in, whole[0], whole[1])


def solution(mesh):
    parts = Mesh(mesh.devices.reshape(Y, ZL, CORE, X, ZH), AXES)
    nodes = P(AXES, None)
    return jax.shard_map(
        local,
        mesh=parts,
        in_specs=(
            nodes, nodes, nodes, nodes, nodes, P(), P(),
            P(ROWS, COLS, None, None, None),
            P(ROWS, COLS, None),
            P(ROWS, COLS),
        ),
        out_specs=(nodes, P(), P()),
        check_vma=False,
    )
```

```python
import jax
import jax.numpy as jnp
import numpy as np
from jax import lax
from jax.experimental import pallas as pl
from jax.experimental.pallas import tpu as pltpu
from jax.sharding import Mesh, PartitionSpec as P

Y, ZL, CORE, X, ZH = 8, 4, 2, 4, 2
AXES = ("y", "zl", "core", "x", "zh")
ROWS = ("y", "zl", "core")
COLS = ("x", "zh")
NCOL = X * ZH
BF16, F32 = jnp.bfloat16, jnp.float32


def everyone(value, axes, count):
    return lax.all_to_all(
        jnp.broadcast_to(value[None], (count,) + value.shape), axes, 0, 0, tiled=True
    )


def y_pairs(which):
    pairs = []
    for y in range(Y):
        for core in range(CORE):
            up = (y + core + which) % 2 == 0
            pairs.append((y * CORE + core, (y + (1 if up else -1)) % Y * CORE + core))
    return pairs


def piece_table():
    step = [dict(y_pairs(0)), dict(y_pairs(1))]
    table = np.zeros((Y * CORE, Y), np.int32)
    for me in range(Y * CORE):
        for piece, hops in enumerate(
            ((), (0,), (1,), (1, 0), (0, 1), (0, 1, 0), (1, 0, 1), (1, 0, 1, 0))
        ):
            at = me
            for hop in hops:
                at = step[hop][at]
            table[me, at // CORE] = piece
    return table


def gather_y(mine, early=None, late=None):
    def swap(value, which):
        return lax.ppermute(value, ("y", "core"), y_pairs(which))

    first, second = swap(mine, 0), swap(mine, 1)
    third, fourth = swap(first, 1), swap(second, 0)
    if early is not None:
        third, early = lax.optimization_barrier((third, early))
    fifth, sixth = swap(third, 0), swap(fourth, 1)
    if late is not None:
        fifth, late = lax.optimization_barrier((fifth, late))
    last = swap(fifth, 1)
    return (mine, first, second, third, fourth, fifth, sixth, last), early, late


def spmm_kernel(meta_ref, table_ref, place_ref, *refs):
    pieces, (own_ref, other_ref, out_ref, x_ref, adj_ref, x_sem, adj_sem) = refs[:Y], refs[Y:]
    core = place_ref[1]
    at = (place_ref[0] * CORE + core) * Y
    per_side, slots = own_ref.shape[0], own_ref.shape[1]
    per_piece = pieces[0].shape[0]
    together = 4
    groups = per_side // together
    empty = x_ref.shape[0] - 1
    x_copies = [
        pltpu.make_async_copy(ref, x_ref.at[pl.ds(p * per_piece, per_piece)], x_sem.at[p])
        for p, ref in enumerate(pieces)
    ]

    def adj_copy(ref, side, m):
        return pltpu.make_async_copy(
            ref.at[pl.ds(m * together, together)],
            adj_ref.at[pl.ds(side * per_side + m * together, together)],
            adj_sem.at[side * groups + m],
        )

    for copy in x_copies:
        copy.start()
    for side, ref in enumerate((own_ref, other_ref)):
        for m in range(groups):
            adj_copy(ref, side, m).start()
    x_ref[empty] = jnp.zeros(x_ref.shape[1:], x_ref.dtype)
    for copy in x_copies:
        copy.wait()

    for side, ref in enumerate((own_ref, other_ref)):
        j = jnp.bitwise_xor(core, side)

        def some_rows(m, carry, side=side, ref=ref, j=j):
            adj_copy(ref, side, m).wait()
            for t in range(together):
                i = m * together + t
                base = (j * per_side + i) * 16
                count = meta_ref[base + slots]
                blocks = []
                for k in range(slots):
                    block = meta_ref[base + k]
                    found = table_ref[at + block // per_piece] * per_piece + block % per_piece
                    blocks.append(x_ref[jnp.where(k < count, found, empty)])
                adj = [adj_ref[side * per_side + i, k] for k in range(slots)]
                out_ref[i, j] = jnp.dot(
                    jnp.concatenate(adj, axis=1),
                    jnp.concatenate(blocks, axis=0),
                    preferred_element_type=F32,
                ).astype(out_ref.dtype)
            return carry

        lax.fori_loop(0, groups, some_rows, 0)


def spmm(meta, place, pieces, own, other):
    smem = pl.BlockSpec(memory_space=pltpu.SMEM)
    anywhere = pl.BlockSpec(memory_space=pl.ANY)
    blocks, bs, half = pieces[0].shape
    rows = own.shape[0] * CORE
    return pl.pallas_call(
        spmm_kernel,
        out_shape=jax.ShapeDtypeStruct((NCOL, CORE, bs, half), BF16),
        in_specs=[smem, smem, smem] + [anywhere] * (Y + 2),
        out_specs=pl.BlockSpec(memory_space=pltpu.VMEM),
        scratch_shapes=[
            pltpu.VMEM((blocks * Y + 1, bs, half), BF16),
            pltpu.VMEM((rows,) + own.shape[1:], BF16),
            pltpu.SemaphoreType.DMA((Y,)),
            pltpu.SemaphoreType.DMA((rows // 4,)),
        ],
        compiler_params=pltpu.CompilerParams(vmem_limit_bytes=60 * 1024 * 1024),
    )(meta, jnp.asarray(piece_table().reshape(-1)), place, *pieces, own, other)


def contract_rows(a, b):
    return lax.dot_general(a, b, (((0,), (0,)), ((), ())), preferred_element_type=F32)


def times_transpose(a, b):
    return lax.dot_general(a, b, (((1,), (1,)), ((), ())), preferred_element_type=F32)


def local(
    grad_out, mask_top, mask_mid, feats_in, feats_mid, weight_first, weight_second,
    adj_blocks, block_cols, block_counts,
):
    bs, feats = grad_out.shape
    half = feats // CORE
    core = lax.axis_index("core")
    nodes = bs * Y * ZL * CORE * X * ZH
    norm_scale = 1.0 / jnp.sqrt(F32(nodes))

    def my_half(v):
        return lax.dynamic_slice_in_dim(v, core * half, half, axis=v.ndim - 1)

    adj = adj_blocks[:, 0]
    meta = jnp.concatenate(
        [block_cols[:, 0], block_counts, jnp.zeros((NCOL, 16 - 13), jnp.int32)], axis=1
    )
    meta = lax.all_gather(meta, "core", axis=0, tiled=True).reshape(-1)
    place = jnp.stack([lax.axis_index("y"), core]).astype(jnp.int32)

    with jax.named_scope("pair_inputs"):
        grad_top = jnp.where(mask_top > 0, grad_out, jnp.zeros_like(grad_out))
        unit_top = my_half(lax.all_gather(grad_top, "core", axis=0, tiled=True))
        pair = lax.all_gather(
            jnp.stack([mask_mid.astype(BF16), feats_mid]), "core", axis=1, tiled=True
        )
        mask_pair = my_half(pair[0])
        feats_mid_pair = pair[1]
    def gather_z(unit):
        return everyone(unit, "zl", ZL).reshape(-1, bs, half)

    with jax.named_scope("section_top"):
        units = gather_z(unit_top)
        mine = lax.all_gather(feats_in, "core", axis=0, tiled=True)
        adj, mine, units = lax.optimization_barrier((adj, mine, units))
        other_adj = lax.ppermute(adj, "core", [(0, 1), (1, 0)])
        other = lax.ppermute(mine, "zh", [(0, 1), (1, 0)])
        pieces, meta, (other_adj, other) = gather_y(units, meta, (other_adj, other))
        partial_top = spmm(meta, place, pieces, adj, other_adj)
        parts = lax.all_to_all(
            partial_top.reshape(NCOL, CORE * bs, half), COLS, 0, 0, tiled=True
        )
        agg_top = jnp.sum(parts.astype(F32), axis=0).astype(BF16)
        agg_top_both = lax.all_gather(agg_top, "core", axis=1, tiled=True)
        term_second = contract_rows(feats_mid_pair, agg_top)
        weight_half = lax.dynamic_slice_in_dim(weight_second, core * half, half, axis=0)
        hidden = times_transpose(agg_top_both, weight_half)
        grad_mid = jnp.where(mask_pair > 0, hidden, jnp.zeros_like(hidden)).astype(BF16)
    with jax.named_scope("section_mid"):
        first_zh = lax.axis_index("zh") == 0
        both = jnp.stack([jnp.where(first_zh, mine, other), jnp.where(first_zh, other, mine)])
        both = jnp.broadcast_to(both[None], (X,) + both.shape)
        units, both = lax.optimization_barrier((gather_z(grad_mid), both))
        feats_in_group = lax.all_to_all(both, "x", 0, 0, tiled=True).reshape(-1, feats)
        partial_mid = spmm(meta, place, gather_y(units)[0], adj, other_adj)
        term_first = contract_rows(feats_in_group, partial_mid.reshape(-1, half))
        terms = jnp.stack([term_first, term_second]).astype(BF16)
        terms = terms.reshape(2, NCOL, feats // NCOL, half).transpose(1, 0, 2, 3)
        sent = jnp.concatenate(
            [partial_mid.reshape(NCOL, CORE * bs, half), terms.reshape(NCOL, -1, half)], axis=1
        )
        parts = lax.all_to_all(sent, COLS, 0, 0, tiled=True)
        summed = jnp.sum(parts.astype(F32), axis=0)
        agg_mid = summed[: CORE * bs].astype(BF16)
        own_nodes = lax.all_gather(agg_mid, "core", axis=1, tiled=True)
        own_nodes = lax.dynamic_slice_in_dim(own_nodes, core * bs, bs, axis=0)
        grad_in = times_transpose(own_nodes, weight_first).astype(BF16)
    with jax.named_scope("weight_sums"):
        piece = summed[CORE * bs :]
        over_y = everyone(piece.astype(BF16), "y", Y)
        piece = jnp.sum(over_y.reshape((Y,) + piece.shape).astype(F32), axis=0)
        over_xz = everyone(piece.astype(BF16), ("x", "zh", "zl"), NCOL * ZL)
        over_x = jnp.sum(over_xz.reshape((NCOL, ZL) + piece.shape).astype(F32), axis=1)
        over_x = over_x.reshape(NCOL, 2, feats // NCOL, half)
        whole = lax.all_gather(over_x * norm_scale, "core", axis=3, tiled=True)
        whole = whole.transpose(1, 0, 2, 3).reshape(2, feats, feats)
    return (grad_in, whole[0], whole[1])


def solution(mesh):
    parts = Mesh(mesh.devices.reshape(Y, ZL, CORE, X, ZH), AXES)
    nodes = P(AXES, None)
    return jax.shard_map(
        local,
        mesh=parts,
        in_specs=(
            nodes, nodes, nodes, nodes, nodes, P(), P(),
            P(ROWS, COLS, None, None, None),
            P(ROWS, COLS, None),
            P(ROWS, COLS),
        ),
        out_specs=(nodes, P(), P()),
        check_vma=False,
    )
```

```python
import jax
import jax.numpy as jnp
import numpy as np
from jax import lax
from jax.experimental import pallas as pl
from jax.experimental.pallas import tpu as pltpu
from jax.sharding import Mesh, PartitionSpec as P

Y, ZL, CORE, X, ZH = 8, 4, 2, 4, 2
AXES = ("y", "zl", "core", "x", "zh")
ROWS = ("y", "zl", "core")
COLS = ("x", "zh")
NCOL = X * ZH
BF16, F32 = jnp.bfloat16, jnp.float32


def everyone(value, axes, count):
    return lax.all_to_all(
        jnp.broadcast_to(value[None], (count,) + value.shape), axes, 0, 0, tiled=True
    )


def y_pairs(which):
    pairs = []
    for y in range(Y):
        for core in range(CORE):
            up = (y + core + which) % 2 == 0
            pairs.append((y * CORE + core, (y + (1 if up else -1)) % Y * CORE + core))
    return pairs


def piece_table():
    step = [dict(y_pairs(0)), dict(y_pairs(1))]
    table = np.zeros((Y * CORE, Y), np.int32)
    for me in range(Y * CORE):
        for piece, hops in enumerate(
            ((), (0,), (1,), (1, 0), (0, 1), (0, 1, 0), (1, 0, 1), (1, 0, 1, 0))
        ):
            at = me
            for hop in hops:
                at = step[hop][at]
            table[me, at // CORE] = piece
    return table


def gather_y(mine, early=None, late=None):
    def swap(value, which):
        return lax.ppermute(value, ("y", "core"), y_pairs(which))

    first, second = swap(mine, 0), swap(mine, 1)
    third, fourth = swap(first, 1), swap(second, 0)
    if early is not None:
        third, early = lax.optimization_barrier((third, early))
    fifth, sixth = swap(third, 0), swap(fourth, 1)
    if late is not None:
        fifth, late = lax.optimization_barrier((fifth, late))
    last = swap(fifth, 1)
    return (mine, first, second, third, fourth, fifth, sixth, last), early, late


def spmm_kernel(meta_ref, table_ref, place_ref, *refs):
    pieces, (own_ref, other_ref, out_ref, x_ref, adj_ref, x_sem, adj_sem) = refs[:Y], refs[Y:]
    core = place_ref[1]
    at = (place_ref[0] * CORE + core) * Y
    per_side, slots = own_ref.shape[0], own_ref.shape[1]
    per_piece = pieces[0].shape[0]
    together = 4
    groups = per_side // together
    empty = x_ref.shape[0] - 1
    x_copies = [
        pltpu.make_async_copy(ref, x_ref.at[pl.ds(p * per_piece, per_piece)], x_sem.at[p])
        for p, ref in enumerate(pieces)
    ]

    def adj_copy(ref, side, m):
        return pltpu.make_async_copy(
            ref.at[pl.ds(m * together, together)],
            adj_ref.at[pl.ds(side * per_side + m * together, together)],
            adj_sem.at[side * groups + m],
        )

    for copy in x_copies:
        copy.start()
    for side, ref in enumerate((own_ref, other_ref)):
        for m in range(groups):
            adj_copy(ref, side, m).start()
    x_ref[empty] = jnp.zeros(x_ref.shape[1:], x_ref.dtype)
    for copy in x_copies:
        copy.wait()

    for side, ref in enumerate((own_ref, other_ref)):
        j = jnp.bitwise_xor(core, side)

        def some_rows(m, carry, side=side, ref=ref, j=j):
            adj_copy(ref, side, m).wait()
            for t in range(together):
                i = m * together + t
                base = (j * per_side + i) * 16
                count = meta_ref[base + slots]
                blocks = []
                for k in range(slots):
                    block = meta_ref[base + k]
                    found = table_ref[at + block // per_piece] * per_piece + block % per_piece
                    blocks.append(x_ref[jnp.where(k < count, found, empty)])
                adj = [adj_ref[side * per_side + i, k] for k in range(slots)]
                out_ref[i, j] = jnp.dot(
                    jnp.concatenate(adj, axis=1),
                    jnp.concatenate(blocks, axis=0),
                    preferred_element_type=F32,
                ).astype(out_ref.dtype)
            return carry

        lax.fori_loop(0, groups, some_rows, 0)


def spmm(meta, place, pieces, own, other):
    smem = pl.BlockSpec(memory_space=pltpu.SMEM)
    anywhere = pl.BlockSpec(memory_space=pl.ANY)
    blocks, bs, half = pieces[0].shape
    rows = own.shape[0] * CORE
    return pl.pallas_call(
        spmm_kernel,
        out_shape=jax.ShapeDtypeStruct((NCOL, CORE, bs, half), BF16),
        in_specs=[smem, smem, smem] + [anywhere] * (Y + 2),
        out_specs=pl.BlockSpec(memory_space=pltpu.VMEM),
        scratch_shapes=[
            pltpu.VMEM((blocks * Y + 1, bs, half), BF16),
            pltpu.VMEM((rows,) + own.shape[1:], BF16),
            pltpu.SemaphoreType.DMA((Y,)),
            pltpu.SemaphoreType.DMA((rows // 4,)),
        ],
        compiler_params=pltpu.CompilerParams(vmem_limit_bytes=60 * 1024 * 1024),
    )(meta, jnp.asarray(piece_table().reshape(-1)), place, *pieces, own, other)


def contract_rows(a, b):
    return lax.dot_general(a, b, (((0,), (0,)), ((), ())), preferred_element_type=F32)


def times_transpose(a, b):
    return lax.dot_general(a, b, (((1,), (1,)), ((), ())), preferred_element_type=F32)


def local(
    grad_out, mask_top, mask_mid, feats_in, feats_mid, weight_first, weight_second,
    adj_blocks, block_cols, block_counts,
):
    bs, feats = grad_out.shape
    half = feats // CORE
    core = lax.axis_index("core")
    nodes = bs * Y * ZL * CORE * X * ZH
    norm_scale = 1.0 / jnp.sqrt(F32(nodes))

    def my_half(v):
        return lax.dynamic_slice_in_dim(v, core * half, half, axis=v.ndim - 1)

    adj = adj_blocks[:, 0]
    meta = jnp.concatenate(
        [block_cols[:, 0], block_counts, jnp.zeros((NCOL, 16 - 13), jnp.int32)], axis=1
    )
    meta = lax.all_gather(meta, "core", axis=0, tiled=True).reshape(-1)
    place = jnp.stack([lax.axis_index("y"), core]).astype(jnp.int32)

    with jax.named_scope("pair_inputs"):
        grad_top = jnp.where(mask_top > 0, grad_out, jnp.zeros_like(grad_out))
        unit_top = my_half(lax.all_gather(grad_top, "core", axis=0, tiled=True))
        pair = lax.all_gather(
            jnp.stack([mask_mid.astype(BF16), feats_mid, feats_in]), "core", axis=1, tiled=True
        )
    def gather_z(unit):
        return everyone(unit, "zl", ZL).reshape(-1, bs, half)

    with jax.named_scope("section_top"):
        units = gather_z(unit_top)
        adj, pair, units = lax.optimization_barrier((adj, pair, units))
        mask_pair, feats_mid_pair, mine = my_half(pair[0]), pair[1], pair[2]
        other_adj = lax.ppermute(adj, "core", [(0, 1), (1, 0)])
        other = lax.ppermute(mine, "zh", [(0, 1), (1, 0)])
        pieces, meta, (other_adj, other) = gather_y(units, meta, (other_adj, other))
        partial_top = spmm(meta, place, pieces, adj, other_adj)
        parts = lax.all_to_all(
            partial_top.reshape(NCOL, CORE * bs, half), COLS, 0, 0, tiled=True
        )
        agg_top = jnp.sum(parts.astype(F32), axis=0).astype(BF16)
        agg_top_both = lax.all_gather(agg_top, "core", axis=1, tiled=True)
        term_second = contract_rows(feats_mid_pair, agg_top)
        weight_half = lax.dynamic_slice_in_dim(weight_second, core * half, half, axis=0)
        hidden = times_transpose(agg_top_both, weight_half)
        grad_mid = jnp.where(mask_pair > 0, hidden, jnp.zeros_like(hidden)).astype(BF16)
    with jax.named_scope("section_mid"):
        first_zh = lax.axis_index("zh") == 0
        both = jnp.concatenate([jnp.where(first_zh, mine, other), jnp.where(first_zh, other, mine)])
        both = jnp.broadcast_to(both[None], (X,) + both.shape)
        units, both = lax.optimization_barrier((gather_z(grad_mid), both))
        feats_in_group = lax.all_to_all(both, "x", 0, 0, tiled=True).reshape(-1, feats)
        partial_mid = spmm(meta, place, gather_y(units)[0], adj, other_adj)
        term_first = contract_rows(feats_in_group, partial_mid.reshape(-1, half))
        terms = jnp.stack([term_first, term_second]).astype(BF16)
        terms = terms.reshape(2, NCOL, feats // NCOL, half).transpose(1, 0, 2, 3)
        sent = jnp.concatenate(
            [partial_mid.reshape(NCOL, CORE * bs, half), terms.reshape(NCOL, -1, half)], axis=1
        )
        parts = lax.all_to_all(sent, COLS, 0, 0, tiled=True)
        summed = jnp.sum(parts.astype(F32), axis=0)
        agg_mid = summed[: CORE * bs].astype(BF16)
        own_nodes = lax.all_gather(agg_mid, "core", axis=1, tiled=True)
        own_nodes = lax.dynamic_slice_in_dim(own_nodes, core * bs, bs, axis=0)
        grad_in = times_transpose(own_nodes, weight_first).astype(BF16)
    with jax.named_scope("weight_sums"):
        piece = summed[CORE * bs :]
        over_y = everyone(piece.astype(BF16), "y", Y)
        piece = jnp.sum(over_y.reshape((Y,) + piece.shape).astype(F32), axis=0)
        over_xz = everyone(piece.astype(BF16), ("x", "zh", "zl"), NCOL * ZL)
        over_x = jnp.sum(over_xz.reshape((NCOL, ZL) + piece.shape).astype(F32), axis=1)
        over_x = over_x.reshape(NCOL, 2, feats // NCOL, half)
        whole = lax.all_gather(over_x * norm_scale, "core", axis=3, tiled=True)
        whole = whole.transpose(1, 0, 2, 3).reshape(2, feats, feats)
    return (grad_in, whole[0], whole[1])


def solution(mesh):
    parts = Mesh(mesh.devices.reshape(Y, ZL, CORE, X, ZH), AXES)
    nodes = P(AXES, None)
    return jax.shard_map(
        local,
        mesh=parts,
        in_specs=(
            nodes, nodes, nodes, nodes, nodes, P(), P(),
            P(ROWS, COLS, None, None, None),
            P(ROWS, COLS, None),
            P(ROWS, COLS),
        ),
        out_specs=(nodes, P(), P()),
        check_vma=False,
    )
```

```python
import jax
import jax.numpy as jnp
import numpy as np
from jax import lax
from jax.experimental import pallas as pl
from jax.experimental.pallas import tpu as pltpu
from jax.sharding import Mesh, PartitionSpec as P

Y, ZL, CORE, X, ZH = 8, 4, 2, 4, 2
AXES = ("y", "zl", "core", "x", "zh")
ROWS = ("y", "zl", "core")
COLS = ("x", "zh")
NCOL = X * ZH
BF16, F32 = jnp.bfloat16, jnp.float32


def everyone(value, axes, count):
    return lax.all_to_all(
        jnp.broadcast_to(value[None], (count,) + value.shape), axes, 0, 0, tiled=True
    )


def y_pairs(which):
    pairs = []
    for y in range(Y):
        for core in range(CORE):
            up = (y + core + which) % 2 == 0
            pairs.append((y * CORE + core, (y + (1 if up else -1)) % Y * CORE + core))
    return pairs


def piece_table():
    step = [dict(y_pairs(0)), dict(y_pairs(1))]
    table = np.zeros((Y * CORE, Y), np.int32)
    for me in range(Y * CORE):
        for piece, hops in enumerate(
            ((), (0,), (1,), (1, 0), (0, 1), (0, 1, 0), (1, 0, 1), (1, 0, 1, 0))
        ):
            at = me
            for hop in hops:
                at = step[hop][at]
            table[me, at // CORE] = piece
    return table


def gather_y(mine, early=None, late=None):
    def swap(value, which):
        return lax.ppermute(value, ("y", "core"), y_pairs(which))

    first, second = swap(mine, 0), swap(mine, 1)
    third, fourth = swap(first, 1), swap(second, 0)
    if early is not None:
        third, early = lax.optimization_barrier((third, early))
    fifth, sixth = swap(third, 0), swap(fourth, 1)
    if late is not None:
        fifth, late = lax.optimization_barrier((fifth, late))
    last = swap(fifth, 1)
    return (mine, first, second, third, fourth, fifth, sixth, last), early, late


def spmm_kernel(meta_ref, table_ref, place_ref, *refs):
    pieces, (own_ref, other_ref, out_ref, x_ref, adj_ref, x_sem, adj_sem) = refs[:Y], refs[Y:]
    core = place_ref[1]
    at = (place_ref[0] * CORE + core) * Y
    per_side, slots = own_ref.shape[0], own_ref.shape[1]
    per_piece = pieces[0].shape[0]
    together = 4
    groups = per_side // together
    empty = x_ref.shape[0] - 1
    x_copies = [
        pltpu.make_async_copy(ref, x_ref.at[pl.ds(p * per_piece, per_piece)], x_sem.at[p])
        for p, ref in enumerate(pieces)
    ]

    def adj_copy(ref, side, m):
        return pltpu.make_async_copy(
            ref.at[pl.ds(m * together, together)],
            adj_ref.at[pl.ds(side * per_side + m * together, together)],
            adj_sem.at[side * groups + m],
        )

    for copy in x_copies:
        copy.start()
    for side, ref in enumerate((own_ref, other_ref)):
        for m in range(groups):
            adj_copy(ref, side, m).start()
    x_ref[empty] = jnp.zeros(x_ref.shape[1:], x_ref.dtype)
    for copy in x_copies:
        copy.wait()

    for side, ref in enumerate((own_ref, other_ref)):
        j = jnp.bitwise_xor(core, side)

        def some_rows(m, carry, side=side, ref=ref, j=j):
            adj_copy(ref, side, m).wait()
            for t in range(together):
                i = m * together + t
                base = (j * per_side + i) * 16
                count = meta_ref[base + slots]
                blocks = []
                for k in range(slots):
                    block = meta_ref[base + k]
                    found = table_ref[at + block // per_piece] * per_piece + block % per_piece
                    blocks.append(x_ref[jnp.where(k < count, found, empty)])
                adj = [adj_ref[side * per_side + i, k] for k in range(slots)]
                out_ref[i, j] = jnp.dot(
                    jnp.concatenate(adj, axis=1),
                    jnp.concatenate(blocks, axis=0),
                    preferred_element_type=F32,
                ).astype(out_ref.dtype)
            return carry

        lax.fori_loop(0, groups, some_rows, 0)


def spmm(meta, place, pieces, own, other):
    smem = pl.BlockSpec(memory_space=pltpu.SMEM)
    anywhere = pl.BlockSpec(memory_space=pl.ANY)
    blocks, bs, half = pieces[0].shape
    rows = own.shape[0] * CORE
    return pl.pallas_call(
        spmm_kernel,
        out_shape=jax.ShapeDtypeStruct((NCOL, CORE, bs, half), BF16),
        in_specs=[smem, smem, smem] + [anywhere] * (Y + 2),
        out_specs=pl.BlockSpec(memory_space=pltpu.VMEM),
        scratch_shapes=[
            pltpu.VMEM((blocks * Y + 1, bs, half), BF16),
            pltpu.VMEM((rows,) + own.shape[1:], BF16),
            pltpu.SemaphoreType.DMA((Y,)),
            pltpu.SemaphoreType.DMA((rows // 4,)),
        ],
        compiler_params=pltpu.CompilerParams(vmem_limit_bytes=60 * 1024 * 1024),
    )(meta, jnp.asarray(piece_table().reshape(-1)), place, *pieces, own, other)


def contract_rows(a, b):
    return lax.dot_general(a, b, (((0,), (0,)), ((), ())), preferred_element_type=F32)


def times_transpose(a, b):
    return lax.dot_general(a, b, (((1,), (1,)), ((), ())), preferred_element_type=F32)


def local(
    grad_out, mask_top, mask_mid, feats_in, feats_mid, weight_first, weight_second,
    adj_blocks, block_cols, block_counts,
):
    bs, feats = grad_out.shape
    half = feats // CORE
    core = lax.axis_index("core")
    nodes = bs * Y * ZL * CORE * X * ZH
    norm_scale = 1.0 / jnp.sqrt(F32(nodes))

    def my_half(v):
        return lax.dynamic_slice_in_dim(v, core * half, half, axis=v.ndim - 1)

    adj = adj_blocks[:, 0]
    meta = jnp.concatenate(
        [block_cols[:, 0], block_counts, jnp.zeros((NCOL, 16 - 13), jnp.int32)], axis=1
    )
    meta = lax.all_gather(meta, "core", axis=0, tiled=True).reshape(-1)
    place = jnp.stack([lax.axis_index("y"), core]).astype(jnp.int32)

    with jax.named_scope("pair_inputs"):
        grad_top = jnp.where(mask_top > 0, grad_out, jnp.zeros_like(grad_out))
        unit_top = my_half(lax.all_gather(grad_top, "core", axis=0, tiled=True))
        pair = lax.all_gather(
            jnp.stack([mask_mid.astype(BF16), feats_mid]), "core", axis=1, tiled=True
        )
        mask_pair = my_half(pair[0])
        feats_mid_pair = pair[1]
    def gather_z(unit):
        return everyone(unit, "zl", ZL).reshape(-1, bs, half)

    with jax.named_scope("section_top"):
        adj, unit_top = lax.optimization_barrier((adj, unit_top))
        other_adj = lax.ppermute(adj, "core", [(0, 1), (1, 0)])
        units = gather_z(unit_top)
        mine = lax.all_gather(feats_in, "core", axis=0, tiled=True)
        mine, units = lax.optimization_barrier((mine, units))
        other = lax.ppermute(mine, "zh", [(0, 1), (1, 0)])
        pieces, meta, (other_adj, other) = gather_y(units, meta, (other_adj, other))
        partial_top = spmm(meta, place, pieces, adj, other_adj)
        parts = lax.all_to_all(
            partial_top.reshape(NCOL, CORE * bs, half), COLS, 0, 0, tiled=True
        )
        agg_top = jnp.sum(parts.astype(F32), axis=0).astype(BF16)
        agg_top_both = lax.all_gather(agg_top, "core", axis=1, tiled=True)
        term_second = contract_rows(feats_mid_pair, agg_top)
        weight_half = lax.dynamic_slice_in_dim(weight_second, core * half, half, axis=0)
        hidden = times_transpose(agg_top_both, weight_half)
        grad_mid = jnp.where(mask_pair > 0, hidden, jnp.zeros_like(hidden)).astype(BF16)
    with jax.named_scope("section_mid"):
        first_zh = lax.axis_index("zh") == 0
        both = jnp.stack([jnp.where(first_zh, mine, other), jnp.where(first_zh, other, mine)])
        both = jnp.broadcast_to(both[None], (X,) + both.shape)
        units, both = lax.optimization_barrier((gather_z(grad_mid), both))
        feats_in_group = lax.all_to_all(both, "x", 0, 0, tiled=True).reshape(-1, feats)
        partial_mid = spmm(meta, place, gather_y(units)[0], adj, other_adj)
        term_first = contract_rows(feats_in_group, partial_mid.reshape(-1, half))
        terms = jnp.stack([term_first, term_second]).astype(BF16)
        terms = terms.reshape(2, NCOL, feats // NCOL, half).transpose(1, 0, 2, 3)
        sent = jnp.concatenate(
            [partial_mid.reshape(NCOL, CORE * bs, half), terms.reshape(NCOL, -1, half)], axis=1
        )
        parts = lax.all_to_all(sent, COLS, 0, 0, tiled=True)
        summed = jnp.sum(parts.astype(F32), axis=0)
        agg_mid = summed[: CORE * bs].astype(BF16)
        own_nodes = lax.all_gather(agg_mid, "core", axis=1, tiled=True)
        own_nodes = lax.dynamic_slice_in_dim(own_nodes, core * bs, bs, axis=0)
        grad_in = times_transpose(own_nodes, weight_first).astype(BF16)
    with jax.named_scope("weight_sums"):
        piece = summed[CORE * bs :]
        over_y = everyone(piece.astype(BF16), "y", Y)
        piece = jnp.sum(over_y.reshape((Y,) + piece.shape).astype(F32), axis=0)
        over_xz = everyone(piece.astype(BF16), ("x", "zh", "zl"), NCOL * ZL)
        over_x = jnp.sum(over_xz.reshape((NCOL, ZL) + piece.shape).astype(F32), axis=1)
        over_x = over_x.reshape(NCOL, 2, feats // NCOL, half)
        whole = lax.all_gather(over_x * norm_scale, "core", axis=3, tiled=True)
        whole = whole.transpose(1, 0, 2, 3).reshape(2, feats, feats)
    return (grad_in, whole[0], whole[1])


def solution(mesh):
    parts = Mesh(mesh.devices.reshape(Y, ZL, CORE, X, ZH), AXES)
    nodes = P(AXES, None)
    return jax.shard_map(
        local,
        mesh=parts,
        in_specs=(
            nodes, nodes, nodes, nodes, nodes, P(), P(),
            P(ROWS, COLS, None, None, None),
            P(ROWS, COLS, None),
            P(ROWS, COLS),
        ),
        out_specs=(nodes, P(), P()),
        check_vma=False,
    )
```
